256 devices in a mesh: slab: 2 (over x_lo), sector: 64 (over x_hi, z, y), side: 2 (over core).
Axes of the slice: x: 4 (x_hi: 2, x_lo: 2; x = x_hi * 2 + x_lo), y: 4, z: 8, core: 2. Of those that a mesh axis runs over, the one named last changes fastest.
Arguments:
- traces: float32 [2, 4096, 4, 512], P('side', 'sector', None, 'slab'), may hold values from -6 to 6
- gap_gain: float32 [1024], replicated, may hold values from 0.2 to 1
- rotor_step: int32 [1], replicated, may hold values from 0 to 4095
- mixing: float32 [2, 3, 4], P('side'), may hold values from -4 to 4
- field: float32 [2, 3, 8, 4096, 512], P('side', None, None, 'sector', 'slab'), may hold values from -6 to 6
- current: float32 [2, 3, 8, 4096, 512], P('side', None, None, 'sector', 'slab'), may hold values from -6 to 6
- cond_diag: float32 [2, 3, 8, 4096, 512], P('side', None, None, 'sector', 'slab'), may hold values from 0.5 to 3
- cond_off: float32 [2, 3, 8, 4096, 512], P('side', None, None, 'sector', 'slab'), may hold values from -0.6 to 0.6
Outputs:
- new_field: float32 [2, 3, 8, 4096, 512], P('side', None, None, 'sector', 'slab')
The draws below stay inside these ranges and needn't reach their ends.
All inputs are finite; a program needn't handle non-finite values.
Results may differ from the reference program's by a relative error of at most 0.000052.
Values sent between devices are 32-bit elements; how exact they have to be, the bound alone decides.
A program may use at most 128 MiB of HBM per device.

```python
import math
import jax
import jax.numpy as jnp
from jax import lax

NPHI = 4096
NH = 1024
COMP = 4
NR = 8
SWEEPS = 2
AX = 512


def steps_of(key, shape, split, least, largest):
    gain = 1.0
    for dim, blocks in split:
        heights = jax.random.uniform(jax.random.fold_in(jax.random.fold_in(key, 6), dim), (blocks,), jnp.float32, least / len(split), largest / len(split))
        gain = gain * jnp.repeat(jnp.exp(heights), shape[dim] // blocks).reshape((-1,) + (1,) * (len(shape) - 1 - dim))
    return gain


def noise(stream_key, shape, spread, most, shards=(), kind=jnp.bfloat16):
    drawn = spread * jax.random.normal(stream_key, shape, jnp.float32)
    if shards:
        drawn = drawn * steps_of(stream_key, shape, shards, -0.22, 0.18)
    return jnp.clip(drawn, -most, most).astype(kind)


def setup_inputs(seed: int = 0) -> dict:
    seeds = jax.random.split(jax.random.key(seed), 9)
    return {
        "traces": noise(seeds[0], (2, NPHI, COMP, AX), 1.0, 6.0, ((0, 2), (1, 64), (3, 2)), jnp.float32),
        "gap_gain": jnp.clip(jnp.exp(jax.random.uniform(seeds[1], (NH,), jnp.float32, math.log(0.2), math.log(1.0))), 0.2, 1.0),
        "rotor_step": jax.random.randint(seeds[2], (1,), 0, NPHI).astype(jnp.int32),
        "mixing": noise(seeds[3], (2, 3, COMP), 1.0, 4.0, ((0, 2),), jnp.float32),
        "field": noise(seeds[4], (2, 3, NR, NPHI, AX), 1.0, 6.0, ((0, 2), (3, 64), (4, 2)), jnp.float32),
        "current": noise(seeds[5], (2, 3, NR, NPHI, AX), 1.0, 6.0, ((0, 2), (3, 64), (4, 2)), jnp.float32),
        "cond_diag": jnp.clip(0.5 + 2.5 * jax.random.uniform(seeds[6], (2, 3, NR, NPHI, AX), jnp.float32) ** steps_of(seeds[6], (2, 3, NR, NPHI, AX), ((0, 2), (3, 64), (4, 2)), -0.2, 0.2), 0.5, 3.0),
        "cond_off": jnp.clip(jax.random.uniform(seeds[7], (2, 3, NR, NPHI, AX), jnp.float32, -0.6, 0.6) * steps_of(seeds[7], (2, 3, NR, NPHI, AX), ((0, 2), (3, 64), (4, 2)), -0.4, 0.0), -0.6, 0.6),
    }


def neighbours(a):
    rad = jnp.pad(a, ((0, 0), (0, 0), (1, 1), (0, 0), (0, 0)))
    total = rad[:, :, 2:] + rad[:, :, :-2]
    total = total + jnp.roll(a, 1, axis=3) + jnp.roll(a, -1, axis=3)
    axial = jnp.pad(a, ((0, 0), (0, 0), (0, 0), (0, 0), (1, 1)))
    return total + axial[..., 2:] + axial[..., :-2]


def reference(traces, gap_gain, rotor_step, mixing, field, current, cond_diag, cond_off):
    spec = jnp.fft.rfft(traces, axis=1)[:, :NH]
    harm = jnp.arange(NH, dtype=jnp.int32)
    angle = ((harm * rotor_step[0]) % NPHI).astype(jnp.float32) * (2.0 * math.pi / NPHI)
    sign = jnp.array([1.0, -1.0], jnp.float32)
    rot = jnp.cos(angle)[None, :] + 1j * (sign[:, None] * jnp.sin(angle)[None, :])
    sent = spec * rot[:, :, None, None]
    coupled = spec + gap_gain[None, :, None, None] * sent[::-1]
    extra = jnp.zeros((2, NPHI // 2 + 1 - NH, COMP, AX), coupled.dtype)
    full = jnp.concatenate([coupled, extra], axis=1)
    wave = jnp.fft.irfft(full, n=NPHI, axis=1).astype(jnp.float32)
    source = jnp.einsum("sck,snka->scna", mixing, wave, precision=lax.Precision.HIGHEST)
    rhs = current.at[:, :, 0].add(source)
    da = 6.0 + cond_diag[:, 0]
    db = 6.0 + cond_diag[:, 1]
    dc = 6.0 + cond_diag[:, 2]
    op, oq, orr = cond_off[:, 0], cond_off[:, 1], cond_off[:, 2]
    c00 = db * dc - orr * orr
    c01 = oq * orr - op * dc
    c02 = op * orr - oq * db
    c11 = da * dc - oq * oq
    c12 = op * oq - da * orr
    c22 = da * db - op * op
    inv_det = 1.0 / (da * c00 + op * c01 + oq * c02)
    potential = field
    for sweep in range(SWEEPS):
        y = rhs + neighbours(potential)
        x0 = (c00 * y[:, 0] + c01 * y[:, 1] + c02 * y[:, 2]) * inv_det
        x1 = (c01 * y[:, 0] + c11 * y[:, 1] + c12 * y[:, 2]) * inv_det
        x2 = (c02 * y[:, 0] + c12 * y[:, 1] + c22 * y[:, 2]) * inv_det
        potential = jnp.stack([x0, x1, x2], axis=1)
    return potential
```

```python
import math

import jax
import jax.numpy as jnp
import ml_dtypes
import numpy as np
from jax import lax
from jax.experimental import pallas as pl
from jax.experimental.pallas import tpu as pltpu
from jax.sharding import PartitionSpec as P

SWEEPS = 2
MESH = pl.DeviceIdType.MESH
SECTORS = 64
PHD = 64
NPHI = 4096
M1 = 16
LAYERS = 8
AXD = 256
F32 = jnp.float32
BF16 = jnp.bfloat16


def split_table(table):
    high = table.astype(np.float32).astype(ml_dtypes.bfloat16)
    low = (table - high.astype(np.float64)).astype(np.float32).astype(ml_dtypes.bfloat16)
    return np.stack([high, low])


def tables():
    s = np.arange(SECTORS)
    m0 = np.arange(64)
    p = np.arange(PHD)
    m1 = np.arange(M1)
    a = 2.0 * np.pi * ((m0[:, None] * s[None, :]) % 64) / 64.0
    outer = np.concatenate([np.cos(a), -np.sin(a)], axis=0)
    b = 2.0 * np.pi * (m0[:, None] * p[None, :]) / NPHI
    twiddle = np.stack([np.tile(np.cos(b), (1, 2)), np.tile(np.sin(b), (1, 2))]).astype(np.float32)
    c = 2.0 * np.pi * ((p[:, None] * m1[None, :]) % 64) / 64.0
    groups = np.eye(8)
    cos_b = np.kron(groups, np.cos(c))
    sin_b = np.kron(groups, np.sin(c))
    inner = np.block([[cos_b, -sin_b], [sin_b, cos_b]])
    pick = np.zeros((3 * 128, 128))
    for k in range(3):
        for qa in range(2):
            pick[k * 128 + qa * 64 + 63, qa * 4 + k] = 1.0
            pick[k * 128 + qa * 64, 8 + qa * 4 + k] = 1.0
    return (
        split_table(outer),
        split_table(np.ascontiguousarray(outer.T)),
        split_table(inner),
        split_table(np.ascontiguousarray(inner.T)),
        twiddle,
        pick.astype(ml_dtypes.bfloat16),
    )


def halves(x):
    high = x.astype(BF16)
    return high, (x - high.astype(F32)).astype(BF16)


def mm(a, b):
    return jnp.dot(a, b, preferred_element_type=F32)


def dot_right(x, table):
    rows = x.shape[0]
    high, low = halves(x)
    both = mm(jnp.concatenate([high, low], axis=0), table[0])
    return both[:rows] + both[rows:] + mm(high, table[1])


def dot_left(table, x):
    high, low = halves(x)
    return mm(table[0], high) + mm(table[0], low) + mm(table[1], high)


def kernel(
    step_ref, mix_ref, gain_ref, traces_hbm, field_hbm, current_hbm, diag_hbm, off_hbm,
    f1_hbm, f2_hbm, g_hbm, h_hbm, tw_hbm, pick_hbm,
    out_hbm,
    traces, field, current, diag, off, f1, f2, g, h, tw, pick,
    dinv, a1, result, wsend, rrecv, usend, urecv, spec, other, etab,
    row_s, row_r, col_s, col_r, row2_s, row2_r, col2_s, col2_r, xcol,
    load, fsend, frecv, usem, ursem, ssend, srecv, hsend, hrecv, h2send, h2recv, xsem, osem,
):
    slab = lax.axis_index("slab")
    me = lax.axis_index("sector")
    side = lax.axis_index("side")
    nxt = lax.rem(me + 1, SECTORS)
    prv = lax.rem(me + SECTORS - 1, SECTORS)

    loads = [
        pltpu.make_async_copy(traces_hbm, traces, load.at[0]),
        pltpu.make_async_copy(field_hbm, field.at[:, pl.ds(1, LAYERS)], load.at[1]),
        pltpu.make_async_copy(diag_hbm, diag, load.at[2]),
        pltpu.make_async_copy(off_hbm, off, load.at[3]),
        pltpu.make_async_copy(current_hbm, current, load.at[4]),
        pltpu.make_async_copy(f1_hbm, f1, load.at[5]),
        pltpu.make_async_copy(f2_hbm, f2, load.at[6]),
        pltpu.make_async_copy(g_hbm, g, load.at[7]),
        pltpu.make_async_copy(h_hbm, h, load.at[8]),
        pltpu.make_async_copy(tw_hbm, tw, load.at[9]),
        pltpu.make_async_copy(pick_hbm, pick, load.at[10]),
    ]
    for copy in loads:
        copy.start()

    barrier = pltpu.get_barrier_semaphore()

    def greet(k, carry):
        pl.semaphore_signal(barrier, inc=1, device_id={"sector": lax.rem(me + k, SECTORS)}, device_id_type=MESH)
        return carry

    pl.semaphore_signal(barrier, inc=1, device_id={"side": 1 - side}, device_id_type=MESH)
    pl.semaphore_signal(barrier, inc=1, device_id={"slab": 1 - slab}, device_id_type=MESH)
    lax.fori_loop(1, SECTORS, greet, 0)

    loads[0].wait()
    for cl in range(2):
        stacked = jnp.concatenate([traces[:, cl, :], traces[:, 2 + cl, :]], axis=0)
        for qa in range(2):
            turned = stacked[:, qa * 128:(qa + 1) * 128].T
            for qb in range(2):
                wsend[pl.ds(cl * 4 + qa * 2 + qb, 64, stride=8), :] = turned[qb * 64:(qb + 1) * 64]

    pl.semaphore_wait(barrier, SECTORS + 1)

    def tile(ref, j):
        return ref.at[pl.ds(pl.multiple_of(j * 8, 8), 8)]

    own = pltpu.make_async_copy(tile(wsend, me), tile(rrecv, me), frecv)
    own.start()

    def scatter(k, carry):
        j = lax.rem(me + k, SECTORS)
        pltpu.make_async_remote_copy(
            src_ref=tile(wsend, j), dst_ref=tile(rrecv, me), send_sem=fsend, recv_sem=frecv,
            device_id={"sector": j}, device_id_type=MESH,
        ).start()
        return carry

    lax.fori_loop(1, SECTORS, scatter, 0)

    lane = lax.broadcasted_iota(jnp.int32, (64, 128), 1)
    wide = lax.broadcasted_iota(jnp.int32, (64, AXD), 1)
    high = lax.broadcasted_iota(jnp.int32, (64, AXD), 0)
    first_slab = slab == 0

    def edge_column(x):
        return jnp.where(first_slab, x[:, AXD - 1:AXD], x[:, 0:1])

    loads[1].wait()
    field[:, 0] = jnp.zeros((3, 64, AXD), F32)
    field[:, LAYERS + 1] = jnp.zeros((3, 64, AXD), F32)
    a1[:, 0] = jnp.zeros((3, 64, AXD), F32)
    a1[:, LAYERS + 1] = jnp.zeros((3, 64, AXD), F32)

    def edges(k, carry):
        columns = col_s[...]
        for c in range(3):
            x = field[c, k + 1]
            row_s[0, pl.ds(c * 8 + k, 1), :] = x[63:64]
            row_s[1, pl.ds(c * 8 + k, 1), :] = x[0:1]
            columns = jnp.where(lane == c * 8 + k, edge_column(x), columns)
        col_s[...] = columns
        return carry

    lax.fori_loop(0, LAYERS, edges, 0)

    def halo(rows_s, rows_r, cols_s, cols_r, send, recv):
        return [
            pltpu.make_async_remote_copy(
                src_ref=rows_s.at[0], dst_ref=rows_r.at[0], send_sem=send.at[0], recv_sem=recv.at[0],
                device_id={"sector": nxt}, device_id_type=MESH,
            ),
            pltpu.make_async_remote_copy(
                src_ref=rows_s.at[1], dst_ref=rows_r.at[1], send_sem=send.at[1], recv_sem=recv.at[1],
                device_id={"sector": prv}, device_id_type=MESH,
            ),
            pltpu.make_async_remote_copy(
                src_ref=cols_s, dst_ref=cols_r, send_sem=send.at[2], recv_sem=recv.at[2],
                device_id={"slab": 1 - slab}, device_id_type=MESH,
            ),
        ]

    halo1 = halo(row_s, row_r, col_s, col_r, hsend, hrecv)
    for copy in halo1:
        copy.start()

    loads[2].wait()
    loads[3].wait()

    def invert(k, carry):
        da = 6.0 + diag[0, k]
        db = 6.0 + diag[1, k]
        dc = 6.0 + diag[2, k]
        op, oq, orr = off[0, k], off[1, k], off[2, k]
        c00 = db * dc - orr * orr
        c01 = oq * orr - op * dc
        c02 = op * orr - oq * db
        c11 = da * dc - oq * oq
        c12 = op * oq - da * orr
        c22 = da * db - op * op
        inv = 1.0 / (da * c00 + op * c01 + oq * c02)
        for i, cof in enumerate((c00, c01, c02, c11, c12, c22)):
            dinv[i, k] = cof * inv
        return carry

    lax.fori_loop(0, LAYERS, invert, 0)

    def solve(k, y):
        d = [dinv[i, k] for i in range(6)]
        return (
            d[0] * y[0] + d[1] * y[1] + d[2] * y[2],
            d[1] * y[0] + d[3] * y[1] + d[4] * y[2],
            d[2] * y[0] + d[4] * y[1] + d[5] * y[2],
        )

    def beside(x, prev_row, next_row, column):
        up = jnp.where(high == 0, prev_row, pltpu.roll(x, 1, 0))
        down = jnp.where(high == 63, next_row, pltpu.roll(x, 63, 0))
        left = jnp.where(wide == 0, jnp.where(first_slab, 0.0, column), pltpu.roll(x, 1, 1))
        right = jnp.where(wide == AXD - 1, jnp.where(first_slab, column, 0.0), pltpu.roll(x, AXD - 1, 1))
        return up + down + (left + right)

    def relax(k, src, rows_r, cols_r):
        y = []
        for c in range(3):
            x = src[c, k + 1]
            column = pltpu.roll(cols_r[...], 128 - c * 8 - k, 1)[:, 0:1]
            near = beside(x, rows_r[0, pl.ds(c * 8 + k, 1), :], rows_r[1, pl.ds(c * 8 + k, 1), :], column)
            y.append(current[c, k] + (src[c, k] + src[c, k + 2] + near))
        return solve(k, y)

    for copy in halo1:
        copy.wait_recv()
    loads[4].wait()

    def sweep1(k, carry):
        new = relax(k, field, row_r, col_r)
        columns = col2_s[...]
        for c in range(3):
            a1[c, k + 1] = new[c]
            row2_s[0, pl.ds(c * 8 + k, 1), :] = new[c][63:64]
            row2_s[1, pl.ds(c * 8 + k, 1), :] = new[c][0:1]
            columns = jnp.where(lane == c * 8 + k, edge_column(new[c]), columns)
        col2_s[...] = columns
        return carry

    lax.fori_loop(0, LAYERS, sweep1, 0)
    columns = col2_s[...]
    for i in range(6):
        x = dinv[i, 0]
        row2_s[0, 24 + i:25 + i, :] = x[63:64]
        row2_s[1, 24 + i:25 + i, :] = x[0:1]
        columns = jnp.where(lane == 24 + i, edge_column(x), columns)
    col2_s[...] = columns
    halo2 = halo(row2_s, row2_r, col2_s, col2_r, h2send, h2recv)
    for copy in halo2:
        copy.start()

    m1 = lane % M1
    harm = lax.broadcasted_iota(jnp.int32, (64, 128), 0) + 64 * m1
    angle = (harm * step_ref[0] % NPHI).astype(F32) * (2.0 * math.pi / NPHI)
    weight = jnp.where(harm == 0, 1.0 / NPHI, 2.0 / NPHI)
    turned = gain_ref[...].T
    gain = jnp.zeros((64, 128), F32)
    for i in range(8):
        gain = jnp.where(m1 == 2 * i, turned[:64, i:i + 1], gain)
        gain = jnp.where(m1 == 2 * i + 1, turned[64:, i:i + 1], gain)
    scaled = gain * weight
    sign = (2 * side - 1).astype(F32)
    etab[0] = weight
    etab[1] = scaled * jnp.cos(angle)
    etab[2] = scaled * jnp.sin(angle) * sign

    for copy in loads[5:]:
        copy.wait()
    pltpu.make_async_copy(wsend, rrecv, frecv).wait()

    exchange = []
    for qb in range(2):
        x = jnp.concatenate([rrecv[pl.ds(2 * r + qb, 64, stride=8), :] for r in range(4)], axis=1)
        y = dot_left(f1, x)
        cos_t = jnp.concatenate([tw[0]] * 4, axis=1)
        sin_t = jnp.concatenate([tw[1]] * 4, axis=1)
        re, im = y[:64], y[64:]
        t = jnp.concatenate([re * cos_t + im * sin_t, im * cos_t - re * sin_t], axis=1)
        spec[qb] = dot_right(t, g)
        copy = pltpu.make_async_remote_copy(
            src_ref=spec.at[qb], dst_ref=other.at[qb], send_sem=ssend.at[qb], recv_sem=srecv.at[qb],
            device_id={"side": 1 - side}, device_id_type=MESH,
        )
        copy.start()
        exchange.append(copy)

    left_half = lane < 64
    for qb in range(2):
        exchange[qb].wait_recv()
        sre, sim = spec[qb, :, :128], spec[qb, :, 128:]
        ore, oim = other[qb, :, :128], other[qb, :, 128:]
        w, ec, es = etab[0], etab[1], etab[2]
        c = jnp.concatenate([w * sre + ec * ore - es * oim, w * sim + ec * oim + es * ore], axis=1)
        z = dot_right(c, h)
        re, im = z[:, :512], z[:, 512:]
        cos_t = jnp.concatenate([tw[0]] * 4, axis=1)
        sin_t = jnp.concatenate([tw[1]] * 4, axis=1)
        x = dot_left(f2, jnp.concatenate([re * cos_t - im * sin_t, im * cos_t + re * sin_t], axis=0))
        packed = []
        for k in range(3):
            coef = [jnp.where(left_half, mix_ref[k, cl], mix_ref[k, 2 + cl]) for cl in range(2)]
            mixed = []
            for qa in range(2):
                v = coef[0] * x[:, qa * 128:(qa + 1) * 128] + coef[1] * x[:, (2 + qa) * 128:(3 + qa) * 128]
                mixed.append(v + pltpu.roll(v, 64, 1))
            packed.append(jnp.where(left_half, mixed[0], mixed[1]))
            usend[pl.ds(2 * k + qb, 64, stride=8), :] = packed[k]
        ph, plow = halves(jnp.concatenate(packed, axis=1))
        ends = mm(ph, pick[...]) + mm(plow, pick[...])
        usend[pl.ds(6 + qb, 64, stride=8), :] = jnp.where(lane < 8, pltpu.roll(ends, 1, 0), pltpu.roll(ends, 63, 0))

    special = jnp.where(first_slab, SECTORS - 1, 0)
    mine = jnp.where(me == special, 1, 0)
    pltpu.make_async_copy(tile(usend, me), tile(urecv, me), ursem.at[mine]).start()

    def gather(k, carry):
        j = lax.rem(me + k, SECTORS)
        pltpu.make_async_remote_copy(
            src_ref=tile(usend, j), dst_ref=tile(urecv, me), send_sem=usem, recv_sem=ursem.at[mine],
            device_id={"sector": j}, device_id_type=MESH,
        ).start()
        return carry

    lax.fori_loop(1, SECTORS, gather, 0)

    for copy in halo2:
        copy.wait_recv()

    def sweep2(k, carry):
        new = relax(k, a1, row2_r, col2_r)
        for c in range(3):
            result[c, k] = new[c]
        return carry

    lax.fori_loop(0, LAYERS, sweep2, 0)
    outs = [pltpu.make_async_copy(result.at[:, pl.ds(2, 6)], out_hbm.at[:, pl.ds(2, 6)], osem.at[0])]
    outs[0].start()

    pltpu.make_async_copy(tile(usend, 0), tile(urecv, 0), ursem.at[1]).wait()
    forward = pltpu.make_async_remote_copy(
        src_ref=tile(urecv, special), dst_ref=xcol, send_sem=xsem.at[0], recv_sem=xsem.at[1],
        device_id={"slab": 1 - slab}, device_id_type=MESH,
    )
    forward.start()
    pltpu.make_async_copy(usend.at[pl.ds(0, 504)], urecv.at[pl.ds(0, 504)], ursem.at[0]).wait()

    turned = []
    for k in range(4):
        both = jnp.concatenate([urecv[pl.ds(2 * k + qb, 64, stride=8), :] for qb in range(2)], axis=0)
        turned.append(both.T)
    source = [jnp.concatenate([turned[c][:64], turned[c][64:]], axis=1) for c in range(3)]
    src_prev = [jnp.concatenate([turned[3][c:c + 1], turned[3][4 + c:5 + c]], axis=1) for c in range(3)]
    src_next = [jnp.concatenate([turned[3][8 + c:9 + c], turned[3][12 + c:13 + c]], axis=1) for c in range(3)]
    delta = solve(0, source)

    def apply(d, y):
        return (
            d[0] * y[0] + d[1] * y[1] + d[2] * y[2],
            d[1] * y[0] + d[3] * y[1] + d[4] * y[2],
            d[2] * y[0] + d[4] * y[1] + d[5] * y[2],
        )

    delta_prev = apply([row2_r[0, 24 + i:25 + i, :] for i in range(6)], src_prev)
    delta_next = apply([row2_r[1, 24 + i:25 + i, :] for i in range(6)], src_next)
    forward.wait_recv()
    cols = xcol[...].T
    cols = [jnp.where(first_slab, cols[:64, 2 * c:2 * c + 1], cols[64:, 2 * c + 1:2 * c + 2]) for c in range(3)]
    dcol = col2_r[...]
    delta_col = apply([dcol[:, 24 + i:25 + i] for i in range(6)], cols)
    y = [source[c] + beside(delta[c], delta_prev[c], delta_next[c], delta_col[c]) for c in range(3)]
    low = solve(0, y)
    up = solve(1, delta)
    for c in range(3):
        result[c, 0] = result[c, 0] + low[c]
        result[c, 1] = result[c, 1] + up[c]
    outs.append(pltpu.make_async_copy(result.at[:, pl.ds(0, 2)], out_hbm.at[:, pl.ds(0, 2)], osem.at[1]))
    outs[1].start()

    pltpu.make_async_copy(wsend.at[pl.ds(0, 504)], rrecv.at[pl.ds(0, 504)], fsend).wait()
    pltpu.make_async_copy(usend.at[pl.ds(0, 504)], urecv.at[pl.ds(0, 504)], usem).wait()
    for copy in halo1 + halo2 + exchange + [forward]:
        copy.wait_send()
    for copy in outs:
        copy.wait()


def shards(traces, gap_gain, rotor_step, mixing, field, current, cond_diag, cond_off):
    consts = [jnp.asarray(t) for t in tables()]
    hbm = pl.BlockSpec(memory_space=pl.ANY)
    smem = pl.BlockSpec(memory_space=pltpu.SMEM)
    vmem = pl.BlockSpec(memory_space=pltpu.VMEM)
    block = (3, LAYERS, PHD, AXD)
    dma = pltpu.SemaphoreType.DMA
    v = pltpu.VMEM
    out = pl.pallas_call(
        kernel,
        out_shape=jax.ShapeDtypeStruct(block, F32),
        in_specs=[smem, smem, vmem] + [hbm] * 11,
        out_specs=hbm,
        scratch_shapes=[
            v((64, 4, AXD), F32), v((3, LAYERS + 2, 64, AXD), F32), v(block, F32), v(block, F32), v(block, F32),
            v((2, 128, 64), BF16), v((2, 64, 128), BF16), v((2, 1024, 256), BF16), v((2, 256, 1024), BF16),
            v((2, 64, 128), F32), v((384, 128), BF16),
            v((6, LAYERS, 64, AXD), F32), v((3, LAYERS + 2, 64, AXD), F32), v(block, F32),
            v((512, 128), F32), v((512, 128), F32), v((512, 128), F32), v((512, 128), F32),
            v((2, 64, 256), F32), v((2, 64, 256), F32), v((3, 64, 128), F32),
            v((2, 24, AXD), F32), v((2, 24, AXD), F32), v((64, 128), F32), v((64, 128), F32),
            v((2, 32, AXD), F32), v((2, 32, AXD), F32), v((64, 128), F32), v((64, 128), F32),
            v((8, 128), F32),
            dma((11,)), dma, dma, dma, dma((2,)), dma((2,)), dma((2,)),
            dma((3,)), dma((3,)), dma((3,)), dma((3,)), dma((2,)), dma((2,)),
        ],
        compiler_params=pltpu.CompilerParams(collective_id=0, has_side_effects=True, vmem_limit_bytes=40 * 1024 * 1024),
        cost_estimate=pl.CostEstimate(flops=400_000_000, bytes_accessed=10_000_000, transcendentals=0),
    )(
        rotor_step, mixing[0], gap_gain.reshape(8, 128), traces[0], field[0], current[0], cond_diag[0], cond_off[0],
        *consts,
    )
    return out[None]


def solution(mesh):
    placed = (
        P("side", "sector", None, "slab"),
        P(),
        P(),
        P("side", None, None),
        P("side", None, None, "sector", "slab"),
        P("side", None, None, "sector", "slab"),
        P("side", None, None, "sector", "slab"),
        P("side", None, None, "sector", "slab"),
    )
    return jax.shard_map(
        shards,
        mesh=mesh,
        in_specs=placed,
        out_specs=P("side", None, None, "sector", "slab"),
        check_vma=False,
    )
```

```python
import math

import jax
import jax.numpy as jnp
import ml_dtypes
import numpy as np
from jax import lax
from jax.experimental import pallas as pl
from jax.experimental.pallas import tpu as pltpu
from jax.sharding import PartitionSpec as P

SWEEPS = 2
MESH = pl.DeviceIdType.MESH
SECTORS = 64
PHD = 64
NPHI = 4096
M1 = 16
LAYERS = 8
AXD = 256
F32 = jnp.float32
BF16 = jnp.bfloat16


def split_table(table):
    high = table.astype(np.float32).astype(ml_dtypes.bfloat16)
    low = (table - high.astype(np.float64)).astype(np.float32).astype(ml_dtypes.bfloat16)
    return np.stack([high, low])


def tables():
    s = np.arange(SECTORS)
    m0 = np.arange(64)
    p = np.arange(PHD)
    m1 = np.arange(M1)
    a = 2.0 * np.pi * ((m0[:, None] * s[None, :]) % 64) / 64.0
    outer = np.concatenate([np.cos(a), -np.sin(a)], axis=0)
    b = 2.0 * np.pi * (m0[:, None] * p[None, :]) / NPHI
    twiddle = np.stack([np.tile(np.cos(b), (1, 2)), np.tile(np.sin(b), (1, 2))]).astype(np.float32)
    c = 2.0 * np.pi * ((p[:, None] * m1[None, :]) % 64) / 64.0
    groups = np.eye(8)
    cos_b = np.kron(groups, np.cos(c))
    sin_b = np.kron(groups, np.sin(c))
    inner = np.block([[cos_b, -sin_b], [sin_b, cos_b]])
    pick = np.zeros((3 * 128, 128))
    for k in range(3):
        for qa in range(2):
            pick[k * 128 + qa * 64 + 63, qa * 4 + k] = 1.0
            pick[k * 128 + qa * 64, 8 + qa * 4 + k] = 1.0
    return (
        split_table(outer),
        split_table(np.ascontiguousarray(outer.T)),
        split_table(inner),
        split_table(np.ascontiguousarray(inner.T)),
        twiddle,
        pick.astype(ml_dtypes.bfloat16),
    )


def halves(x):
    high = x.astype(BF16)
    return high, (x - high.astype(F32)).astype(BF16)


def mm(a, b):
    return jnp.dot(a, b, preferred_element_type=F32)


def dot_right(x, table):
    rows = x.shape[0]
    high, low = halves(x)
    both = mm(jnp.concatenate([high, low], axis=0), table[0])
    return both[:rows] + both[rows:] + mm(high, table[1])


def dot_left(table, x):
    high, low = halves(x)
    return mm(table[0], high) + mm(table[0], low) + mm(table[1], high)


def kernel(
    step_hbm, mix_hbm, gain_hbm, traces_hbm, field_hbm, current_hbm, diag_hbm, off_hbm,
    f1_hbm, f2_hbm, g_hbm, h_hbm, tw_hbm, pick_hbm,
    result,
    step_ref, mix_ref, gain_ref, traces, field, current, diag, off, f1, f2, g, h, tw, pick,
    dinv, a1, wsend, rrecv, usend, urecv, spec, other, etab,
    row_s, row_r, col_s, col_r, row2_s, row2_r, col2_s, col2_r, xcol,
    load, fsend, frecv, usem, ursem, ssend, srecv, hsend, hrecv, h2send, h2recv, xsem,
):
    slab = lax.axis_index("slab")
    me = lax.axis_index("sector")
    side = lax.axis_index("side")
    nxt = lax.rem(me + 1, SECTORS)
    prv = lax.rem(me + SECTORS - 1, SECTORS)

    loads = [
        pltpu.make_async_copy(traces_hbm, traces, load.at[0]),
        pltpu.make_async_copy(field_hbm, field.at[:, pl.ds(1, LAYERS)], load.at[1]),
        pltpu.make_async_copy(diag_hbm, diag, load.at[2]),
        pltpu.make_async_copy(off_hbm, off, load.at[3]),
        pltpu.make_async_copy(current_hbm, current, load.at[4]),
        pltpu.make_async_copy(f1_hbm, f1, load.at[5]),
        pltpu.make_async_copy(f2_hbm, f2, load.at[6]),
        pltpu.make_async_copy(g_hbm, g, load.at[7]),
        pltpu.make_async_copy(h_hbm, h, load.at[8]),
        pltpu.make_async_copy(tw_hbm, tw, load.at[9]),
        pltpu.make_async_copy(pick_hbm, pick, load.at[10]),
        pltpu.make_async_copy(step_hbm, step_ref, load.at[11]),
        pltpu.make_async_copy(mix_hbm, mix_ref, load.at[12]),
        pltpu.make_async_copy(gain_hbm, gain_ref, load.at[13]),
    ]
    for copy in loads:
        copy.start()

    barrier = pltpu.get_barrier_semaphore()

    def turn(k):
        return lax.rem(me + 18 + k, SECTORS)

    def greet(k, carry):
        pl.semaphore_signal(barrier, inc=1, device_id={"slab": 1 - slab, "sector": turn(k)}, device_id_type=MESH)
        return carry

    lax.fori_loop(0, SECTORS, greet, 0)
    pl.semaphore_signal(barrier, inc=1, device_id={"side": 1 - side}, device_id_type=MESH)
    pl.semaphore_signal(barrier, inc=1, device_id={"sector": nxt}, device_id_type=MESH)
    pl.semaphore_signal(barrier, inc=1, device_id={"sector": prv}, device_id_type=MESH)

    loads[0].wait()
    for cl in range(2):
        stacked = jnp.concatenate([traces[:, cl, :], traces[:, 2 + cl, :]], axis=0)
        for qa in range(2):
            turned = stacked[:, qa * 128:(qa + 1) * 128].T
            for qb in range(2):
                wsend[pl.ds(cl * 4 + qa * 2 + qb, 64, stride=8), :] = turned[qb * 64:(qb + 1) * 64]

    def tile(ref, j):
        return ref.at[pl.ds(pl.multiple_of(j * 8, 8), 8)]

    lane = lax.broadcasted_iota(jnp.int32, (64, 128), 1)
    wide = lax.broadcasted_iota(jnp.int32, (64, AXD), 1)
    high = lax.broadcasted_iota(jnp.int32, (64, AXD), 0)
    first_slab = slab == 0

    def edge_column(x):
        return jnp.where(first_slab, x[:, AXD - 1:AXD], x[:, 0:1])

    loads[1].wait()
    field[:, 0] = jnp.zeros((3, 64, AXD), F32)
    field[:, LAYERS + 1] = jnp.zeros((3, 64, AXD), F32)
    a1[:, 0] = jnp.zeros((3, 64, AXD), F32)
    a1[:, LAYERS + 1] = jnp.zeros((3, 64, AXD), F32)

    def edges(k, carry):
        columns = col_s[...]
        for c in range(3):
            x = field[c, k + 1]
            row_s[0, pl.ds(c * 8 + k, 1), :] = x[63:64]
            row_s[1, pl.ds(c * 8 + k, 1), :] = x[0:1]
            columns = jnp.where(lane == c * 8 + k, edge_column(x), columns)
        col_s[...] = columns
        return carry

    lax.fori_loop(0, LAYERS, edges, 0)

    def halo(rows_s, rows_r, cols_s, cols_r, send, recv):
        return [
            pltpu.make_async_remote_copy(
                src_ref=rows_s.at[0], dst_ref=rows_r.at[0], send_sem=send.at[0], recv_sem=recv.at[0],
                device_id={"sector": nxt}, device_id_type=MESH,
            ),
            pltpu.make_async_remote_copy(
                src_ref=rows_s.at[1], dst_ref=rows_r.at[1], send_sem=send.at[1], recv_sem=recv.at[1],
                device_id={"sector": prv}, device_id_type=MESH,
            ),
            pltpu.make_async_remote_copy(
                src_ref=cols_s, dst_ref=cols_r, send_sem=send.at[2], recv_sem=recv.at[2],
                device_id={"slab": 1 - slab}, device_id_type=MESH,
            ),
        ]

    pl.semaphore_wait(barrier, SECTORS + 3)

    halo1 = halo(row_s, row_r, col_s, col_r, hsend, hrecv)
    for copy in halo1:
        copy.start()

    def scatter(k, carry):
        j = turn(k)
        pltpu.make_async_remote_copy(
            src_ref=tile(wsend, j), dst_ref=tile(rrecv, me), send_sem=fsend, recv_sem=frecv,
            device_id={"slab": 1 - slab, "sector": j}, device_id_type=MESH,
        ).start()
        return carry

    lax.fori_loop(0, SECTORS, scatter, 0)

    loads[2].wait()
    loads[3].wait()

    def invert(k, carry):
        da = 6.0 + diag[0, k]
        db = 6.0 + diag[1, k]
        dc = 6.0 + diag[2, k]
        op, oq, orr = off[0, k], off[1, k], off[2, k]
        c00 = db * dc - orr * orr
        c01 = oq * orr - op * dc
        c02 = op * orr - oq * db
        c11 = da * dc - oq * oq
        c12 = op * oq - da * orr
        c22 = da * db - op * op
        inv = 1.0 / (da * c00 + op * c01 + oq * c02)
        for i, cof in enumerate((c00, c01, c02, c11, c12, c22)):
            dinv[i, k] = cof * inv
        return carry

    lax.fori_loop(0, LAYERS, invert, 0)

    def solve(k, y):
        d = [dinv[i, k] for i in range(6)]
        return (
            d[0] * y[0] + d[1] * y[1] + d[2] * y[2],
            d[1] * y[0] + d[3] * y[1] + d[4] * y[2],
            d[2] * y[0] + d[4] * y[1] + d[5] * y[2],
        )

    def beside(x, prev_row, next_row, column):
        up = jnp.where(high == 0, prev_row, pltpu.roll(x, 1, 0))
        down = jnp.where(high == 63, next_row, pltpu.roll(x, 63, 0))
        left = jnp.where(wide == 0, jnp.where(first_slab, 0.0, column), pltpu.roll(x, 1, 1))
        right = jnp.where(wide == AXD - 1, jnp.where(first_slab, column, 0.0), pltpu.roll(x, AXD - 1, 1))
        return up + down + (left + right)

    def relax(k, src, rows_r, cols_r):
        y = []
        for c in range(3):
            x = src[c, k + 1]
            column = pltpu.roll(cols_r[...], 128 - c * 8 - k, 1)[:, 0:1]
            near = beside(x, rows_r[0, pl.ds(c * 8 + k, 1), :], rows_r[1, pl.ds(c * 8 + k, 1), :], column)
            y.append(current[c, k] + (src[c, k] + src[c, k + 2] + near))
        return solve(k, y)

    for copy in halo1:
        copy.wait_recv()
    loads[4].wait()

    def sweep1(k, carry):
        new = relax(k, field, row_r, col_r)
        columns = col2_s[...]
        for c in range(3):
            a1[c, k + 1] = new[c]
            row2_s[0, pl.ds(c * 8 + k, 1), :] = new[c][63:64]
            row2_s[1, pl.ds(c * 8 + k, 1), :] = new[c][0:1]
            columns = jnp.where(lane == c * 8 + k, edge_column(new[c]), columns)
        col2_s[...] = columns
        return carry

    lax.fori_loop(0, LAYERS, sweep1, 0)
    columns = col2_s[...]
    for i in range(6):
        x = dinv[i, 0]
        row2_s[0, 24 + i:25 + i, :] = x[63:64]
        row2_s[1, 24 + i:25 + i, :] = x[0:1]
        columns = jnp.where(lane == 24 + i, edge_column(x), columns)
    col2_s[...] = columns
    halo2 = halo(row2_s, row2_r, col2_s, col2_r, h2send, h2recv)
    for copy in halo2:
        copy.start()

    for copy in loads[11:]:
        copy.wait()

    m1 = lane % M1
    harm = lax.broadcasted_iota(jnp.int32, (64, 128), 0) + 64 * m1
    angle = (harm * step_ref[0] % NPHI).astype(F32) * (2.0 * math.pi / NPHI)
    weight = jnp.where(harm == 0, 1.0 / NPHI, 2.0 / NPHI)
    turned = gain_ref[...].T
    gain = jnp.zeros((64, 128), F32)
    for i in range(8):
        gain = jnp.where(m1 == 2 * i, turned[:64, i:i + 1], gain)
        gain = jnp.where(m1 == 2 * i + 1, turned[64:, i:i + 1], gain)
    scaled = gain * weight
    sign = (2 * side - 1).astype(F32)
    etab[0] = weight
    etab[1] = scaled * jnp.cos(angle)
    etab[2] = scaled * jnp.sin(angle) * sign

    for copy in loads[5:11]:
        copy.wait()
    pltpu.make_async_copy(wsend, rrecv, frecv).wait()

    exchange = []
    for qb in range(2):
        x = jnp.concatenate([rrecv[pl.ds(2 * r + qb, 64, stride=8), :] for r in range(4)], axis=1)
        y = dot_left(f1, x)
        cos_t = jnp.concatenate([tw[0]] * 4, axis=1)
        sin_t = jnp.concatenate([tw[1]] * 4, axis=1)
        re, im = y[:64], y[64:]
        t = jnp.concatenate([re * cos_t + im * sin_t, im * cos_t - re * sin_t], axis=1)
        spec[qb] = dot_right(t, g)
        copy = pltpu.make_async_remote_copy(
            src_ref=spec.at[qb], dst_ref=other.at[qb], send_sem=ssend.at[qb], recv_sem=srecv.at[qb],
            device_id={"side": 1 - side}, device_id_type=MESH,
        )
        copy.start()
        exchange.append(copy)

    left_half = lane < 64
    for qb in range(2):
        exchange[qb].wait_recv()
        sre, sim = spec[qb, :, :128], spec[qb, :, 128:]
        ore, oim = other[qb, :, :128], other[qb, :, 128:]
        w, ec, es = etab[0], etab[1], etab[2]
        c = jnp.concatenate([w * sre + ec * ore - es * oim, w * sim + ec * oim + es * ore], axis=1)
        z = dot_right(c, h)
        re, im = z[:, :512], z[:, 512:]
        cos_t = jnp.concatenate([tw[0]] * 4, axis=1)
        sin_t = jnp.concatenate([tw[1]] * 4, axis=1)
        x = dot_left(f2, jnp.concatenate([re * cos_t - im * sin_t, im * cos_t + re * sin_t], axis=0))
        packed = []
        for k in range(3):
            coef = [jnp.where(left_half, mix_ref[k, 0, cl], mix_ref[k, 0, 2 + cl]) for cl in range(2)]
            mixed = []
            for qa in range(2):
                v = coef[0] * x[:, qa * 128:(qa + 1) * 128] + coef[1] * x[:, (2 + qa) * 128:(3 + qa) * 128]
                mixed.append(v + pltpu.roll(v, 64, 1))
            packed.append(jnp.where(left_half, mixed[0], mixed[1]))
            usend[pl.ds(2 * k + qb, 64, stride=8), :] = packed[k]
        ph, plow = halves(jnp.concatenate(packed, axis=1))
        ends = mm(ph, pick[...]) + mm(plow, pick[...])
        usend[pl.ds(6 + qb, 64, stride=8), :] = jnp.where(lane < 8, pltpu.roll(ends, 1, 0), pltpu.roll(ends, 63, 0))

    special = jnp.where(first_slab, SECTORS - 1, 0)
    mine = jnp.where(me == SECTORS - 1 - special, 1, 0)

    def gather(k, carry):
        j = turn(k)
        pltpu.make_async_remote_copy(
            src_ref=tile(usend, j), dst_ref=tile(urecv, me), send_sem=usem, recv_sem=ursem.at[mine],
            device_id={"slab": 1 - slab, "sector": j}, device_id_type=MESH,
        ).start()
        return carry

    lax.fori_loop(0, SECTORS, gather, 0)

    for copy in halo2:
        copy.wait_recv()

    def sweep2(k, carry):
        new = relax(k, a1, row2_r, col2_r)
        for c in range(3):
            result[c, k] = new[c]
        return carry

    lax.fori_loop(0, LAYERS, sweep2, 0)

    pltpu.make_async_copy(tile(usend, 0), tile(urecv, 0), ursem.at[1]).wait()
    forward = pltpu.make_async_remote_copy(
        src_ref=tile(urecv, special), dst_ref=xcol, send_sem=xsem.at[0], recv_sem=xsem.at[1],
        device_id={"slab": 1 - slab}, device_id_type=MESH,
    )
    forward.start()
    pltpu.make_async_copy(usend.at[pl.ds(0, 504)], urecv.at[pl.ds(0, 504)], ursem.at[0]).wait()

    turned = []
    for k in range(4):
        both = jnp.concatenate([urecv[pl.ds(2 * k + qb, 64, stride=8), :] for qb in range(2)], axis=0)
        turned.append(both.T)
    source = [jnp.concatenate([turned[c][:64], turned[c][64:]], axis=1) for c in range(3)]
    src_prev = [jnp.concatenate([turned[3][c:c + 1], turned[3][4 + c:5 + c]], axis=1) for c in range(3)]
    src_next = [jnp.concatenate([turned[3][8 + c:9 + c], turned[3][12 + c:13 + c]], axis=1) for c in range(3)]
    delta = solve(0, source)

    def apply(d, y):
        return (
            d[0] * y[0] + d[1] * y[1] + d[2] * y[2],
            d[1] * y[0] + d[3] * y[1] + d[4] * y[2],
            d[2] * y[0] + d[4] * y[1] + d[5] * y[2],
        )

    delta_prev = apply([row2_r[0, 24 + i:25 + i, :] for i in range(6)], src_prev)
    delta_next = apply([row2_r[1, 24 + i:25 + i, :] for i in range(6)], src_next)
    forward.wait_recv()
    cols = xcol[...].T
    cols = [jnp.where(first_slab, cols[:64, 2 * c:2 * c + 1], cols[64:, 2 * c + 1:2 * c + 2]) for c in range(3)]
    dcol = col2_r[...]
    delta_col = apply([dcol[:, 24 + i:25 + i] for i in range(6)], cols)
    y = [source[c] + beside(delta[c], delta_prev[c], delta_next[c], delta_col[c]) for c in range(3)]
    low = solve(0, y)
    up = solve(1, delta)
    for c in range(3):
        result[c, 0] = result[c, 0] + low[c]
        result[c, 1] = result[c, 1] + up[c]

    pltpu.make_async_copy(wsend, rrecv, fsend).wait()
    pltpu.make_async_copy(usend, urecv, usem).wait()
    for copy in halo1 + halo2 + exchange + [forward]:
        copy.wait_send()


def shards(traces, gap_gain, rotor_step, mixing, field, current, cond_diag, cond_off):
    consts = [jnp.asarray(t) for t in tables()]
    hbm = pl.BlockSpec(memory_space=pltpu.HBM)
    vmem = pl.BlockSpec(memory_space=pltpu.VMEM)
    block = (3, LAYERS, PHD, AXD)
    dma = pltpu.SemaphoreType.DMA
    v = pltpu.VMEM
    out = pl.pallas_call(
        kernel,
        out_shape=jax.ShapeDtypeStruct(block, F32),
        in_specs=[hbm] * 14,
        out_specs=vmem,
        scratch_shapes=[
            pltpu.SMEM((1,), jnp.int32), pltpu.SMEM((3, 1, 4), F32), v((8, 128), F32),
            v((64, 4, AXD), F32), v((3, LAYERS + 2, 64, AXD), F32), v(block, F32), v(block, F32), v(block, F32),
            v((2, 128, 64), BF16), v((2, 64, 128), BF16), v((2, 1024, 256), BF16), v((2, 256, 1024), BF16),
            v((2, 64, 128), F32), v((384, 128), BF16),
            v((6, LAYERS, 64, AXD), F32), v((3, LAYERS + 2, 64, AXD), F32),
            v((512, 128), F32), v((512, 128), F32), v((512, 128), F32), v((512, 128), F32),
            v((2, 64, 256), F32), v((2, 64, 256), F32), v((3, 64, 128), F32),
            v((2, 24, AXD), F32), v((2, 24, AXD), F32), v((64, 128), F32), v((64, 128), F32),
            v((2, 32, AXD), F32), v((2, 32, AXD), F32), v((64, 128), F32), v((64, 128), F32),
            v((8, 128), F32),
            dma((14,)), dma, dma, dma, dma((2,)), dma((2,)), dma((2,)),
            dma((3,)), dma((3,)), dma((3,)), dma((3,)), dma((2,)),
        ],
        compiler_params=pltpu.CompilerParams(collective_id=0, has_side_effects=True, vmem_limit_bytes=62 * 1024 * 1024),
        cost_estimate=pl.CostEstimate(flops=400_000_000, bytes_accessed=10_000_000, transcendentals=0),
    )(
        rotor_step, jnp.transpose(mixing, (1, 0, 2)), gap_gain.reshape(8, 128), traces[0], field[0], current[0], cond_diag[0], cond_off[0],
        *consts,
    )
    return out[None]


def solution(mesh):
    placed = (
        P("side", "sector", None, "slab"),
        P(),
        P(),
        P("side", None, None),
        P("side", None, None, "sector", "slab"),
        P("side", None, None, "sector", "slab"),
        P("side", None, None, "sector", "slab"),
        P("side", None, None, "sector", "slab"),
    )
    return jax.shard_map(
        shards,
        mesh=mesh,
        in_specs=placed,
        out_specs=P("side", None, None, "sector", "slab"),
        check_vma=False,
    )
```

```python
import math

import jax
import jax.numpy as jnp
import ml_dtypes
import numpy as np
from jax import lax
from jax.experimental import pallas as pl
from jax.experimental.pallas import tpu as pltpu
from jax.sharding import PartitionSpec as P

SWEEPS = 2
MESH = pl.DeviceIdType.MESH
SECTORS = 64
PHD = 64
NPHI = 4096
M1 = 16
LAYERS = 8
AXD = 256
F32 = jnp.float32
BF16 = jnp.bfloat16


def split_table(table):
    high = table.astype(np.float32).astype(ml_dtypes.bfloat16)
    low = (table - high.astype(np.float64)).astype(np.float32).astype(ml_dtypes.bfloat16)
    return np.stack([high, low])


def tables():
    s = np.arange(SECTORS)
    m0 = np.arange(64)
    p = np.arange(PHD)
    m1 = np.arange(M1)
    a = 2.0 * np.pi * ((m0[:, None] * s[None, :]) % 64) / 64.0
    outer = np.concatenate([np.cos(a), -np.sin(a)], axis=0)
    b = 2.0 * np.pi * (m0[:, None] * p[None, :]) / NPHI
    twiddle = np.stack([np.tile(np.cos(b), (1, 2)), np.tile(np.sin(b), (1, 2))]).astype(np.float32)
    c = 2.0 * np.pi * ((p[:, None] * m1[None, :]) % 64) / 64.0
    cos_b = np.kron(np.eye(2), np.cos(c))
    sin_b = np.kron(np.eye(2), np.sin(c))
    inner = np.block([[cos_b, -sin_b], [sin_b, cos_b]])
    back = np.concatenate([inner.T, np.zeros((64, 256))], axis=0)
    pick = np.zeros((3 * 128, 128))
    for k in range(3):
        for qa in range(2):
            pick[k * 128 + qa * 64 + 63, qa * 4 + k] = 1.0
            pick[k * 128 + qa * 64, 8 + qa * 4 + k] = 1.0
    return (
        split_table(outer),
        split_table(np.ascontiguousarray(outer.T)),
        split_table(np.tile(inner, (1, 2))),
        split_table(back),
        twiddle,
        pick.astype(ml_dtypes.bfloat16),
    )


def halves(x):
    high = x.astype(BF16)
    return high, (x - high.astype(F32)).astype(BF16)


def mm(a, b):
    return jnp.dot(a, b, preferred_element_type=F32)


def dot_right(x, table):
    rows = x.shape[0]
    high, low = halves(x)
    both = mm(jnp.concatenate([high, low], axis=0), table[0])
    return both[:rows] + both[rows:] + mm(high, table[1])


def dot_left(table, x):
    high, low = halves(x)
    return mm(table[0], high) + mm(table[0], low) + mm(table[1], high)


def apply(d, y):
    return (
        d[0] * y[0] + d[1] * y[1] + d[2] * y[2],
        d[1] * y[0] + d[3] * y[1] + d[4] * y[2],
        d[2] * y[0] + d[4] * y[1] + d[5] * y[2],
    )


def beside(first_slab, x, prev_row, next_row, column):
    wide = lax.broadcasted_iota(jnp.int32, (64, AXD), 1)
    high = lax.broadcasted_iota(jnp.int32, (64, AXD), 0)
    up = jnp.where(high == 0, prev_row, pltpu.roll(x, 1, 0))
    down = jnp.where(high == 63, next_row, pltpu.roll(x, 63, 0))
    left = jnp.where(wide == 0, jnp.where(first_slab, 0.0, column), pltpu.roll(x, 1, 1))
    right = jnp.where(wide == AXD - 1, jnp.where(first_slab, column, 0.0), pltpu.roll(x, AXD - 1, 1))
    return up + down + (left + right)


def kernel(
    step_hbm, mix_hbm, gain_hbm, traces_hbm, field_hbm, current_hbm, diag_hbm, off_hbm,
    f1_hbm, f2_hbm, g_hbm, h_hbm, tw_hbm, pick_hbm,
    out_a, out_u, out_x, out_d, out_r, out_c,
    step_ref, mix_ref, gain_ref, traces, field, current, diag, off, f1, f2, g, h, tw, pick,
    dinv, a1, result, wsend, rrecv, usend, spec, other, etab,
    row_s, row_r, col_s, col_r, row2_s, row2_r, col2_s, col2_r,
    load, fsend, frecv, usem, ursem, ssend, srecv, hsend, hrecv, h2send, h2recv, xsem, osem,
):
    slab = lax.axis_index("slab")
    me = lax.axis_index("sector")
    side = lax.axis_index("side")
    nxt = lax.rem(me + 1, SECTORS)
    prv = lax.rem(me + SECTORS - 1, SECTORS)

    loads = [
        pltpu.make_async_copy(traces_hbm, traces, load.at[0]),
        pltpu.make_async_copy(field_hbm, field.at[:, pl.ds(1, LAYERS)], load.at[1]),
        pltpu.make_async_copy(diag_hbm, diag, load.at[2]),
        pltpu.make_async_copy(off_hbm, off, load.at[3]),
        pltpu.make_async_copy(current_hbm, current, load.at[4]),
        pltpu.make_async_copy(f1_hbm, f1, load.at[5]),
        pltpu.make_async_copy(f2_hbm, f2, load.at[6]),
        pltpu.make_async_copy(g_hbm, g, load.at[7]),
        pltpu.make_async_copy(h_hbm, h, load.at[8]),
        pltpu.make_async_copy(tw_hbm, tw, load.at[9]),
        pltpu.make_async_copy(pick_hbm, pick, load.at[10]),
        pltpu.make_async_copy(step_hbm, step_ref, load.at[11]),
        pltpu.make_async_copy(mix_hbm, mix_ref, load.at[12]),
        pltpu.make_async_copy(gain_hbm, gain_ref, load.at[13]),
    ]
    for copy in loads:
        copy.start()

    barrier = pltpu.get_barrier_semaphore()

    mx, mz, my = me >> 5, (me >> 2) & 7, me & 3
    corners = [x << 5 | (my + d) & 3 for d in (2, 1, 3, 0) for x in (mx, 1 - mx)]

    def each_peer(act):
        def ring(i, carry):
            dx = ((i & 1) ^ mx) << 5
            base = dx | ((my + (i >> 1) + 2) & 3)
            for dz in (4, 3, 5, 2, 6, 1, 7, 0):
                act(base | ((mz + dz) & 7) << 2)
            return carry

        lax.fori_loop(0, 8, ring, 0)

    def greet(j):
        pl.semaphore_signal(barrier, inc=1, device_id={"slab": 1 - slab, "sector": j}, device_id_type=MESH)

    each_peer(greet)
    pl.semaphore_signal(barrier, inc=1, device_id={"side": 1 - side}, device_id_type=MESH)
    pl.semaphore_signal(barrier, inc=1, device_id={"sector": nxt}, device_id_type=MESH)
    pl.semaphore_signal(barrier, inc=1, device_id={"sector": prv}, device_id_type=MESH)

    loads[0].wait()
    for cl in range(2):
        stacked = jnp.concatenate([traces[:, cl, :], traces[:, 2 + cl, :]], axis=0)
        for qa in range(2):
            turned = stacked[:, qa * 128:(qa + 1) * 128].T
            for qb in range(2):
                wsend[pl.ds(cl * 4 + qa * 2 + qb, 64, stride=8), :] = turned[qb * 64:(qb + 1) * 64]

    def tile(ref, j):
        return ref.at[pl.ds(pl.multiple_of(j * 8, 8), 8)]

    lane = lax.broadcasted_iota(jnp.int32, (64, 128), 1)
    first_slab = slab == 0

    def edge_column(x):
        return jnp.where(first_slab, x[:, AXD - 1:AXD], x[:, 0:1])

    loads[1].wait()
    field[:, 0] = jnp.zeros((3, 64, AXD), F32)
    field[:, LAYERS + 1] = jnp.zeros((3, 64, AXD), F32)
    a1[:, 0] = jnp.zeros((3, 64, AXD), F32)
    a1[:, LAYERS + 1] = jnp.zeros((3, 64, AXD), F32)

    def edges(k, carry):
        columns = col_s[...]
        for c in range(3):
            x = field[c, k + 1]
            row_s[0, pl.ds(c * 8 + k, 1), :] = x[63:64]
            row_s[1, pl.ds(c * 8 + k, 1), :] = x[0:1]
            columns = jnp.where(lane == c * 8 + k, edge_column(x), columns)
        col_s[...] = columns
        return carry

    lax.fori_loop(0, LAYERS, edges, 0)

    def halo(rows_s, rows_r, cols_s, cols_r, send, recv):
        return [
            pltpu.make_async_remote_copy(
                src_ref=rows_s.at[0], dst_ref=rows_r.at[0], send_sem=send.at[0], recv_sem=recv.at[0],
                device_id={"sector": nxt}, device_id_type=MESH,
            ),
            pltpu.make_async_remote_copy(
                src_ref=rows_s.at[1], dst_ref=rows_r.at[1], send_sem=send.at[1], recv_sem=recv.at[1],
                device_id={"sector": prv}, device_id_type=MESH,
            ),
            pltpu.make_async_remote_copy(
                src_ref=cols_s, dst_ref=cols_r, send_sem=send.at[2], recv_sem=recv.at[2],
                device_id={"slab": 1 - slab}, device_id_type=MESH,
            ),
        ]

    pl.semaphore_wait(barrier, SECTORS + 3)

    halo1 = halo(row_s, row_r, col_s, col_r, hsend, hrecv)
    for copy in halo1:
        copy.start()

    def scatter(j):
        pltpu.make_async_remote_copy(
            src_ref=tile(wsend, j), dst_ref=tile(rrecv, me), send_sem=fsend, recv_sem=frecv,
            device_id={"slab": 1 - slab, "sector": j}, device_id_type=MESH,
        ).start()

    each_peer(scatter)

    loads[2].wait()
    loads[3].wait()

    def invert(k, carry):
        da = 6.0 + diag[0, k]
        db = 6.0 + diag[1, k]
        dc = 6.0 + diag[2, k]
        op, oq, orr = off[0, k], off[1, k], off[2, k]
        c00 = db * dc - orr * orr
        c01 = oq * orr - op * dc
        c02 = op * orr - oq * db
        c11 = da * dc - oq * oq
        c12 = op * oq - da * orr
        c22 = da * db - op * op
        inv = 1.0 / (da * c00 + op * c01 + oq * c02)
        for i, cof in enumerate((c00, c01, c02, c11, c12, c22)):
            dinv[i, k] = cof * inv
        return carry

    lax.fori_loop(0, LAYERS, invert, 0)

    def solve(k, y):
        return apply([dinv[i, k] for i in range(6)], y)

    def relax(k, src, rows_r, cols_r):
        y = []
        for c in range(3):
            x = src[c, k + 1]
            column = pltpu.roll(cols_r[...], 128 - c * 8 - k, 1)[:, 0:1]
            near = beside(first_slab, x, rows_r[0, pl.ds(c * 8 + k, 1), :], rows_r[1, pl.ds(c * 8 + k, 1), :], column)
            y.append(current[c, k] + (src[c, k] + src[c, k + 2] + near))
        return solve(k, y)

    for copy in halo1:
        copy.wait_recv()
    loads[4].wait()

    def sweep1(k, carry):
        new = relax(k, field, row_r, col_r)
        columns = col2_s[...]
        for c in range(3):
            a1[c, k + 1] = new[c]
            row2_s[0, pl.ds(c * 8 + k, 1), :] = new[c][63:64]
            row2_s[1, pl.ds(c * 8 + k, 1), :] = new[c][0:1]
            columns = jnp.where(lane == c * 8 + k, edge_column(new[c]), columns)
        col2_s[...] = columns
        return carry

    lax.fori_loop(0, LAYERS, sweep1, 0)
    columns = col2_s[...]
    for i in range(6):
        x = dinv[i, 0]
        row2_s[0, 24 + i:25 + i, :] = x[63:64]
        row2_s[1, 24 + i:25 + i, :] = x[0:1]
        columns = jnp.where(lane == 24 + i, edge_column(x), columns)
    col2_s[...] = columns
    halo2 = halo(row2_s, row2_r, col2_s, col2_r, h2send, h2recv)
    for copy in halo2:
        copy.start()

    for copy in loads[11:]:
        copy.wait()

    m1 = lane % M1
    harm = lax.broadcasted_iota(jnp.int32, (64, 128), 0) + 64 * m1
    angle = (harm * step_ref[0] % NPHI).astype(F32) * (2.0 * math.pi / NPHI)
    weight = jnp.where(harm == 0, 1.0 / NPHI, 2.0 / NPHI)
    turned = gain_ref[...].T
    gain = jnp.zeros((64, 128), F32)
    for i in range(8):
        gain = jnp.where(m1 == 2 * i, turned[:64, i:i + 1], gain)
        gain = jnp.where(m1 == 2 * i + 1, turned[64:, i:i + 1], gain)
    scaled = gain * weight
    sign = (2 * side - 1).astype(F32)
    etab[0] = weight
    etab[1] = scaled * jnp.cos(angle)
    etab[2] = scaled * jnp.sin(angle) * jnp.where(lane % 64 < 32, -sign, sign)

    for copy in loads[5:11]:
        copy.wait()
    pltpu.make_async_copy(wsend, rrecv, frecv).wait()

    exchange = []
    cos_t, sin_t = tw[0], tw[1]
    left_half = lane < 64
    real_lane = lane % 64 < 32
    batch = 2
    for b in range(2 // batch):
        order = [(cl, qa, qb) for qb in range(batch * b, batch * b + batch) for cl in range(2) for qa in range(2)]
        x = jnp.concatenate([rrecv[pl.ds(cl * 4 + qa * 2 + qb, 64, stride=8), :] for cl, qa, qb in order], axis=1)
        y = dot_left(f1, x)
        rows = []
        for n in range(4 * batch):
            re, im = y[:64, n * 128:n * 128 + 128], y[64:, n * 128:n * 128 + 128]
            rows.append(jnp.concatenate([re * cos_t + im * sin_t, im * cos_t - re * sin_t], axis=1))
        both = dot_right(jnp.concatenate(rows, axis=0), g)
        for n in range(2 * batch):
            spec[2 * batch * b + n] = jnp.where(left_half, both[n * 128:n * 128 + 64], both[n * 128 + 64:n * 128 + 128])
        part = pl.ds(2 * batch * b, 2 * batch)
        copy = pltpu.make_async_remote_copy(
            src_ref=spec.at[part], dst_ref=other.at[part], send_sem=ssend.at[b], recv_sem=srecv.at[b],
            device_id={"side": 1 - side}, device_id_type=MESH,
        )
        copy.start()
        exchange.append(copy)

    for b in range(2 // batch):
        exchange[b].wait_recv()
        rows = []
        for n in range(2 * batch * b, 2 * batch * b + 2 * batch):
            o = other[n]
            crossed = jnp.where(real_lane, pltpu.roll(o, 96, 1), pltpu.roll(o, 32, 1))
            c = etab[0] * spec[n] + etab[1] * o + etab[2] * crossed
            rows += [c, pltpu.roll(c, 64, 1)]
        z = dot_right(jnp.concatenate(rows, axis=0), h)
        parts = []
        for n in range(4 * batch):
            re, im = z[n * 64:n * 64 + 64, :128], z[n * 64:n * 64 + 64, 128:]
            parts.append(jnp.concatenate([re * cos_t - im * sin_t, im * cos_t + re * sin_t], axis=0))
        wave = dot_left(f2, jnp.concatenate(parts, axis=1))
        for q in range(batch):
            qb = b * batch + q
            packed = []
            for k in range(3):
                coef = [jnp.where(left_half, mix_ref[k, 0, cl], mix_ref[k, 0, 2 + cl]) for cl in range(2)]
                mixed = []
                for qa in range(2):
                    at = [(q * 4 + cl * 2 + qa) * 128 for cl in range(2)]
                    v = coef[0] * wave[:, at[0]:at[0] + 128] + coef[1] * wave[:, at[1]:at[1] + 128]
                    mixed.append(v + pltpu.roll(v, 64, 1))
                packed.append(jnp.where(left_half, mixed[0], mixed[1]))
                usend[pl.ds(2 * k + qb, 64, stride=8), :] = packed[k]
            ph, plow = halves(jnp.concatenate(packed, axis=1))
            ends = mm(ph, pick[...]) + mm(plow, pick[...])
            usend[pl.ds(6 + qb, 64, stride=8), :] = jnp.where(lane < 8, pltpu.roll(ends, 1, 0), pltpu.roll(ends, 63, 0))

    special = jnp.where(first_slab, SECTORS - 1, 0)
    mine = jnp.where(me == SECTORS - 1 - special, 1, 0)

    def gather(j):
        pltpu.make_async_remote_copy(
            src_ref=tile(usend, j), dst_ref=tile(out_u, me), send_sem=usem, recv_sem=ursem.at[mine],
            device_id={"slab": 1 - slab, "sector": j}, device_id_type=MESH,
        ).start()

    each_peer(gather)

    for copy in halo2:
        copy.wait_recv()
    outs = [
        pltpu.make_async_copy(dinv.at[:, pl.ds(0, 2)], out_d, osem.at[0]),
        pltpu.make_async_copy(row2_r, out_r, osem.at[1]),
        pltpu.make_async_copy(col2_r, out_c, osem.at[2]),
        pltpu.make_async_copy(result, out_a, osem.at[3]),
    ]
    for copy in outs[:3]:
        copy.start()

    def sweep2(k, carry):
        new = relax(k, a1, row2_r, col2_r)
        for c in range(3):
            result[c, k] = new[c]
        return carry

    lax.fori_loop(0, LAYERS, sweep2, 0)
    outs[3].start()

    pltpu.make_async_copy(tile(usend, 0), tile(out_u, 0), ursem.at[1]).wait()
    forward = pltpu.make_async_remote_copy(
        src_ref=tile(out_u, special), dst_ref=out_x, send_sem=xsem.at[0], recv_sem=xsem.at[1],
        device_id={"slab": 1 - slab}, device_id_type=MESH,
    )
    forward.start()
    pltpu.make_async_copy(usend.at[pl.ds(0, 504)], out_u.at[pl.ds(0, 504)], ursem.at[0]).wait()

    forward.wait_recv()
    pltpu.make_async_copy(wsend, rrecv, fsend).wait()
    pltpu.make_async_copy(usend, out_u, usem).wait()
    for copy in outs:
        copy.wait()
    for copy in halo1 + halo2 + exchange + [forward]:
        copy.wait_send()


def finish(a_hbm, u_hbm, x_hbm, d_hbm, r_hbm, c_hbm, out, result, urecv, xcol, dinv, rows, cols_r, isem, osem):
    first_slab = lax.axis_index("slab") == 0
    loads = [
        pltpu.make_async_copy(src, dst, isem.at[i])
        for i, (src, dst) in enumerate(((u_hbm, urecv), (d_hbm, dinv), (x_hbm, xcol), (r_hbm, rows), (c_hbm, cols_r)))
    ]
    layers = [pl.ds(k, 2) for k in range(0, LAYERS, 2)]
    loads += [pltpu.make_async_copy(a_hbm.at[:, k], result.at[:, k], isem.at[5 + i]) for i, k in enumerate(layers)]
    stores = [pltpu.make_async_copy(result.at[:, k], out.at[:, k], osem.at[i]) for i, k in enumerate(layers)]
    for copy in loads:
        copy.start()
    for i in range(1, 4):
        loads[5 + i].wait()
        stores[i].start()
    for copy in loads[:6]:
        copy.wait()

    def solve(k, y):
        return apply([dinv[i, k] for i in range(6)], y)

    turned = []
    for k in range(4):
        both = jnp.concatenate([urecv[pl.ds(2 * k + qb, 64, stride=8), :] for qb in range(2)], axis=0)
        turned.append(both.T)
    source = [jnp.concatenate([turned[c][:64], turned[c][64:]], axis=1) for c in range(3)]
    src_prev = [jnp.concatenate([turned[3][c:c + 1], turned[3][4 + c:5 + c]], axis=1) for c in range(3)]
    src_next = [jnp.concatenate([turned[3][8 + c:9 + c], turned[3][12 + c:13 + c]], axis=1) for c in range(3)]
    delta = solve(0, source)

    delta_prev = apply([rows[0, 24 + i:25 + i, :] for i in range(6)], src_prev)
    delta_next = apply([rows[1, 24 + i:25 + i, :] for i in range(6)], src_next)
    cols = xcol[...].T
    cols = [jnp.where(first_slab, cols[:64, 2 * c:2 * c + 1], cols[64:, 2 * c + 1:2 * c + 2]) for c in range(3)]
    dcol = cols_r[...]
    delta_col = apply([dcol[:, 24 + i:25 + i] for i in range(6)], cols)
    y = [source[c] + beside(first_slab, delta[c], delta_prev[c], delta_next[c], delta_col[c]) for c in range(3)]
    low = solve(0, y)
    up = solve(1, delta)
    for c in range(3):
        result[c, 0] = result[c, 0] + low[c]
        result[c, 1] = result[c, 1] + up[c]
    stores[0].start()
    for copy in stores:
        copy.wait()


def shards(traces, gap_gain, rotor_step, mixing, field, current, cond_diag, cond_off):
    consts = [jnp.asarray(t) for t in tables()]
    hbm = pl.BlockSpec(memory_space=pltpu.HBM)
    block = (3, LAYERS, PHD, AXD)
    dma = pltpu.SemaphoreType.DMA
    v = pltpu.VMEM
    shapes = (block, (512, 128), (8, 128), (6, 2, 64, AXD), (2, 32, AXD), (64, 128))
    parts = pl.pallas_call(
        kernel,
        out_shape=[jax.ShapeDtypeStruct(shape, F32) for shape in shapes],
        in_specs=[hbm] * 14,
        out_specs=[hbm] * 6,
        scratch_shapes=[
            pltpu.SMEM((1,), jnp.int32), pltpu.SMEM((3, 1, 4), F32), v((8, 128), F32),
            v((64, 4, AXD), F32), v((3, LAYERS + 2, 64, AXD), F32), v(block, F32), v(block, F32), v(block, F32),
            v((2, 128, 64), BF16), v((2, 64, 128), BF16), v((2, 256, 128), BF16), v((2, 128, 256), BF16),
            v((2, 64, 128), F32), v((384, 128), BF16),
            v((6, LAYERS, 64, AXD), F32), v((3, LAYERS + 2, 64, AXD), F32), v(block, F32),
            v((512, 128), F32), v((512, 128), F32), v((512, 128), F32),
            v((4, 64, 128), F32), v((4, 64, 128), F32), v((3, 64, 128), F32),
            v((2, 24, AXD), F32), v((2, 24, AXD), F32), v((64, 128), F32), v((64, 128), F32),
            v((2, 32, AXD), F32), v((2, 32, AXD), F32), v((64, 128), F32), v((64, 128), F32),
            dma((14,)), dma, dma, dma, dma((2,)), dma((4,)), dma((4,)),
            dma((3,)), dma((3,)), dma((3,)), dma((3,)), dma((2,)), dma((4,)),
        ],
        compiler_params=pltpu.CompilerParams(collective_id=0, has_side_effects=True, vmem_limit_bytes=62 * 1024 * 1024),
        cost_estimate=pl.CostEstimate(flops=400_000_000, bytes_accessed=10_000_000, transcendentals=0),
    )(
        rotor_step, jnp.transpose(mixing, (1, 0, 2)), gap_gain.reshape(8, 128), traces[0], field[0], current[0], cond_diag[0], cond_off[0],
        *consts,
    )
    out = pl.pallas_call(
        finish,
        out_shape=jax.ShapeDtypeStruct(block, F32),
        in_specs=[hbm] * 6,
        out_specs=hbm,
        scratch_shapes=[v(shape, F32) for shape in shapes] + [dma((9,)), dma((4,))],
        compiler_params=pltpu.CompilerParams(vmem_limit_bytes=62 * 1024 * 1024),
        cost_estimate=pl.CostEstimate(flops=10_000_000, bytes_accessed=4_200_000, transcendentals=0),
    )(*parts)
    return out[None]


def solution(mesh):
    placed = (
        P("side", "sector", None, "slab"),
        P(),
        P(),
        P("side", None, None),
        P("side", None, None, "sector", "slab"),
        P("side", None, None, "sector", "slab"),
        P("side", None, None, "sector", "slab"),
        P("side", None, None, "sector", "slab"),
    )
    return jax.shard_map(
        shards,
        mesh=mesh,
        in_specs=placed,
        out_specs=P("side", None, None, "sector", "slab"),
        check_vma=False,
    )
```

```python
import math

import jax
import jax.numpy as jnp
import ml_dtypes
import numpy as np
from jax import lax
from jax.experimental import pallas as pl
from jax.experimental.pallas import tpu as pltpu
from jax.sharding import PartitionSpec as P

SWEEPS = 2
MESH = pl.DeviceIdType.MESH
SECTORS = 64
PHD = 64
NPHI = 4096
M1 = 16
LAYERS = 8
AXD = 256
F32 = jnp.float32
BF16 = jnp.bfloat16


def split_table(table):
    high = table.astype(np.float32).astype(ml_dtypes.bfloat16)
    low = (table - high.astype(np.float64)).astype(np.float32).astype(ml_dtypes.bfloat16)
    return np.stack([high, low])


def tables():
    s = np.arange(SECTORS)
    m0 = np.arange(64)
    p = np.arange(PHD)
    m1 = np.arange(M1)
    a = 2.0 * np.pi * ((m0[:, None] * s[None, :]) % 64) / 64.0
    outer = np.concatenate([np.cos(a), -np.sin(a)], axis=0)
    b = 2.0 * np.pi * (m0[:, None] * p[None, :]) / NPHI
    twiddle = np.stack([np.tile(np.cos(b), (1, 2)), np.tile(np.sin(b), (1, 2))]).astype(np.float32)
    c = 2.0 * np.pi * ((p[:, None] * m1[None, :]) % 64) / 64.0
    cos_b = np.kron(np.eye(2), np.cos(c))
    sin_b = np.kron(np.eye(2), np.sin(c))
    inner = np.block([[cos_b, -sin_b], [sin_b, cos_b]])
    back = np.concatenate([inner.T, np.zeros((64, 256))], axis=0)
    pick = np.zeros((3 * 128, 128))
    for k in range(3):
        for qa in range(2):
            pick[k * 128 + qa * 64 + 63, qa * 4 + k] = 1.0
            pick[k * 128 + qa * 64, 8 + qa * 4 + k] = 1.0
    return (
        split_table(outer),
        split_table(np.ascontiguousarray(outer.T)),
        split_table(np.tile(inner, (1, 2))),
        split_table(back),
        twiddle,
        pick.astype(ml_dtypes.bfloat16),
    )


def halves(x):
    high = x.astype(BF16)
    return high, (x - high.astype(F32)).astype(BF16)


def mm(a, b):
    return jnp.dot(a, b, preferred_element_type=F32)


def dot_right(x, table):
    rows = x.shape[0]
    high, low = halves(x)
    both = mm(jnp.concatenate([high, low], axis=0), table[0])
    return both[:rows] + both[rows:] + mm(high, table[1])


def dot_left(table, x):
    high, low = halves(x)
    return mm(table[0], high) + mm(table[0], low) + mm(table[1], high)


def apply(d, y):
    return (
        d[0] * y[0] + d[1] * y[1] + d[2] * y[2],
        d[1] * y[0] + d[3] * y[1] + d[4] * y[2],
        d[2] * y[0] + d[4] * y[1] + d[5] * y[2],
    )


def beside(first_slab, x, prev_row, next_row, column):
    wide = lax.broadcasted_iota(jnp.int32, (64, AXD), 1)
    high = lax.broadcasted_iota(jnp.int32, (64, AXD), 0)
    up = jnp.where(high == 0, prev_row, pltpu.roll(x, 1, 0))
    down = jnp.where(high == 63, next_row, pltpu.roll(x, 63, 0))
    left = jnp.where(wide == 0, jnp.where(first_slab, 0.0, column), pltpu.roll(x, 1, 1))
    right = jnp.where(wide == AXD - 1, jnp.where(first_slab, column, 0.0), pltpu.roll(x, AXD - 1, 1))
    return up + down + (left + right)


def kernel(
    step_hbm, mix_hbm, gain_hbm, traces_hbm, field_hbm, current_hbm, diag_hbm, off_hbm,
    f1_hbm, f2_hbm, g_hbm, h_hbm, tw_hbm, pick_hbm,
    out_a, out_u, out_x, out_d, out_r, out_c,
    step_ref, mix_ref, gain_ref, traces, field, current, diag, off, f1, f2, g, h, tw, pick,
    dinv, a1, result, wsend, rrecv, usend, spec, other, etab,
    row_s, row_r, col_s, col_r, row2_s, row2_r, col2_s, col2_r,
    load, fsend, frecv, usem, ursem, ssend, srecv, hsend, hrecv, h2send, h2recv, xsem, osem,
):
    slab = lax.axis_index("slab")
    me = lax.axis_index("sector")
    side = lax.axis_index("side")
    nxt = lax.rem(me + 1, SECTORS)
    prv = lax.rem(me + SECTORS - 1, SECTORS)

    loads = [
        pltpu.make_async_copy(traces_hbm, traces, load.at[0]),
        pltpu.make_async_copy(field_hbm, field.at[:, pl.ds(1, LAYERS)], load.at[1]),
        pltpu.make_async_copy(diag_hbm, diag, load.at[2]),
        pltpu.make_async_copy(off_hbm, off, load.at[3]),
        pltpu.make_async_copy(current_hbm, current, load.at[4]),
        pltpu.make_async_copy(f1_hbm, f1, load.at[5]),
        pltpu.make_async_copy(f2_hbm, f2, load.at[6]),
        pltpu.make_async_copy(g_hbm, g, load.at[7]),
        pltpu.make_async_copy(h_hbm, h, load.at[8]),
        pltpu.make_async_copy(tw_hbm, tw, load.at[9]),
        pltpu.make_async_copy(pick_hbm, pick, load.at[10]),
        pltpu.make_async_copy(step_hbm, step_ref, load.at[11]),
        pltpu.make_async_copy(mix_hbm, mix_ref, load.at[12]),
        pltpu.make_async_copy(gain_hbm, gain_ref, load.at[13]),
    ]
    for copy in loads:
        copy.start()

    barrier = pltpu.get_barrier_semaphore()

    mx, mz, my = me >> 5, (me >> 2) & 7, me & 3
    corners = [x << 5 | (my + d) & 3 for d in (2, 1, 3, 0) for x in (mx, 1 - mx)]

    def each_peer(act):
        def ring(i, carry):
            dx = ((i & 1) ^ mx) << 5
            base = dx | ((my + (i >> 1) + 2) & 3)
            for dz in (4, 3, 5, 2, 6, 1, 7, 0):
                act(base | ((mz + dz) & 7) << 2)
            return carry

        lax.fori_loop(0, 8, ring, 0)

    def greet(j):
        pl.semaphore_signal(barrier, inc=1, device_id={"slab": 1 - slab, "sector": j}, device_id_type=MESH)

    each_peer(greet)
    pl.semaphore_signal(barrier, inc=1, device_id={"side": 1 - side}, device_id_type=MESH)
    pl.semaphore_signal(barrier, inc=1, device_id={"sector": nxt}, device_id_type=MESH)
    pl.semaphore_signal(barrier, inc=1, device_id={"sector": prv}, device_id_type=MESH)

    loads[0].wait()
    for cl in range(2):
        stacked = jnp.concatenate([traces[:, cl, :], traces[:, 2 + cl, :]], axis=0)
        for qa in range(2):
            turned = stacked[:, qa * 128:(qa + 1) * 128].T
            for qb in range(2):
                wsend[pl.ds(cl * 4 + qa * 2 + qb, 64, stride=8), :] = turned[qb * 64:(qb + 1) * 64]

    def tile(ref, j, rows=8):
        return ref.at[pl.ds(pl.multiple_of(j * 8, 8), rows)]

    lane = lax.broadcasted_iota(jnp.int32, (64, 128), 1)
    first_slab = slab == 0

    def edge_column(x):
        return jnp.where(first_slab, x[:, AXD - 1:AXD], x[:, 0:1])

    loads[1].wait()
    field[:, 0] = jnp.zeros((3, 64, AXD), F32)
    field[:, LAYERS + 1] = jnp.zeros((3, 64, AXD), F32)
    a1[:, 0] = jnp.zeros((3, 64, AXD), F32)
    a1[:, LAYERS + 1] = jnp.zeros((3, 64, AXD), F32)

    def edges(k, carry):
        columns = col_s[...]
        for c in range(3):
            x = field[c, k + 1]
            row_s[0, pl.ds(c * 8 + k, 1), :] = x[63:64]
            row_s[1, pl.ds(c * 8 + k, 1), :] = x[0:1]
            columns = jnp.where(lane == c * 8 + k, edge_column(x), columns)
        col_s[...] = columns
        return carry

    lax.fori_loop(0, LAYERS, edges, 0)

    def halo(rows_s, rows_r, cols_s, cols_r, send, recv):
        return [
            pltpu.make_async_remote_copy(
                src_ref=rows_s.at[0], dst_ref=rows_r.at[0], send_sem=send.at[0], recv_sem=recv.at[0],
                device_id={"sector": nxt}, device_id_type=MESH,
            ),
            pltpu.make_async_remote_copy(
                src_ref=rows_s.at[1], dst_ref=rows_r.at[1], send_sem=send.at[1], recv_sem=recv.at[1],
                device_id={"sector": prv}, device_id_type=MESH,
            ),
            pltpu.make_async_remote_copy(
                src_ref=cols_s, dst_ref=cols_r, send_sem=send.at[2], recv_sem=recv.at[2],
                device_id={"slab": 1 - slab}, device_id_type=MESH,
            ),
        ]

    pl.semaphore_wait(barrier, SECTORS + 3)

    halo1 = halo(row_s, row_r, col_s, col_r, hsend, hrecv)
    for copy in halo1:
        copy.start()

    def scatter(j):
        pltpu.make_async_remote_copy(
            src_ref=tile(wsend, j), dst_ref=tile(rrecv, me), send_sem=fsend, recv_sem=frecv,
            device_id={"slab": 1 - slab, "sector": j}, device_id_type=MESH,
        ).start()

    each_peer(scatter)

    loads[2].wait()
    loads[3].wait()

    def invert(k, carry):
        da = 6.0 + diag[0, k]
        db = 6.0 + diag[1, k]
        dc = 6.0 + diag[2, k]
        op, oq, orr = off[0, k], off[1, k], off[2, k]
        c00 = db * dc - orr * orr
        c01 = oq * orr - op * dc
        c02 = op * orr - oq * db
        c11 = da * dc - oq * oq
        c12 = op * oq - da * orr
        c22 = da * db - op * op
        inv = 1.0 / (da * c00 + op * c01 + oq * c02)
        for i, cof in enumerate((c00, c01, c02, c11, c12, c22)):
            dinv[i, k] = cof * inv
        return carry

    lax.fori_loop(0, LAYERS, invert, 0)

    def solve(k, y):
        return apply([dinv[i, k] for i in range(6)], y)

    def relax(k, src, rows_r, cols_r):
        y = []
        for c in range(3):
            x = src[c, k + 1]
            column = pltpu.roll(cols_r[...], 128 - c * 8 - k, 1)[:, 0:1]
            near = beside(first_slab, x, rows_r[0, pl.ds(c * 8 + k, 1), :], rows_r[1, pl.ds(c * 8 + k, 1), :], column)
            y.append(current[c, k] + (src[c, k] + src[c, k + 2] + near))
        return solve(k, y)

    for copy in halo1:
        copy.wait_recv()
    loads[4].wait()

    def sweep1(k, carry):
        new = relax(k, field, row_r, col_r)
        columns = col2_s[...]
        for c in range(3):
            a1[c, k + 1] = new[c]
            row2_s[0, pl.ds(c * 8 + k, 1), :] = new[c][63:64]
            row2_s[1, pl.ds(c * 8 + k, 1), :] = new[c][0:1]
            columns = jnp.where(lane == c * 8 + k, edge_column(new[c]), columns)
        col2_s[...] = columns
        return carry

    lax.fori_loop(0, LAYERS, sweep1, 0)
    columns = col2_s[...]
    for i in range(6):
        x = dinv[i, 0]
        row2_s[0, 24 + i:25 + i, :] = x[63:64]
        row2_s[1, 24 + i:25 + i, :] = x[0:1]
        columns = jnp.where(lane == 24 + i, edge_column(x), columns)
    col2_s[...] = columns
    halo2 = halo(row2_s, row2_r, col2_s, col2_r, h2send, h2recv)

    for copy in loads[11:]:
        copy.wait()

    m1 = lane % M1
    harm = lax.broadcasted_iota(jnp.int32, (64, 128), 0) + 64 * m1
    angle = (harm * step_ref[0, 0] % NPHI).astype(F32) * (2.0 * math.pi / NPHI)
    weight = jnp.where(harm == 0, 1.0 / NPHI, 2.0 / NPHI)
    turned = gain_ref[...].T
    gain = jnp.zeros((64, 128), F32)
    for i in range(8):
        gain = jnp.where(m1 == 2 * i, turned[:64, i:i + 1], gain)
        gain = jnp.where(m1 == 2 * i + 1, turned[64:, i:i + 1], gain)
    scaled = gain * weight
    sign = (2 * side - 1).astype(F32)
    etab[0] = weight
    etab[1] = scaled * jnp.cos(angle)
    etab[2] = scaled * jnp.sin(angle) * jnp.where(lane % 64 < 32, -sign, sign)

    for copy in loads[5:11]:
        copy.wait()
    pltpu.make_async_copy(wsend, rrecv, frecv).wait()
    for copy in halo2:
        copy.start()

    exchange = []
    edge = []
    cos_t, sin_t = tw[0], tw[1]
    left_half = lane < 64
    real_lane = lane % 64 < 32
    batch = 2
    for b in range(2 // batch):
        order = [(cl, qa, qb) for qb in range(batch * b, batch * b + batch) for cl in range(2) for qa in range(2)]
        x = jnp.concatenate([rrecv[pl.ds(cl * 4 + qa * 2 + qb, 64, stride=8), :] for cl, qa, qb in order], axis=1)
        y = dot_left(f1, x)
        rows = []
        for n in range(4 * batch):
            re, im = y[:64, n * 128:n * 128 + 128], y[64:, n * 128:n * 128 + 128]
            rows.append(jnp.concatenate([re * cos_t + im * sin_t, im * cos_t - re * sin_t], axis=1))
        both = dot_right(jnp.concatenate(rows, axis=0), g)
        for n in range(2 * batch):
            spec[2 * batch * b + n] = jnp.where(left_half, both[n * 128:n * 128 + 64], both[n * 128 + 64:n * 128 + 128])
        part = pl.ds(2 * batch * b, 2 * batch)
        copy = pltpu.make_async_remote_copy(
            src_ref=spec.at[part], dst_ref=other.at[part], send_sem=ssend.at[b], recv_sem=srecv.at[b],
            device_id={"side": 1 - side}, device_id_type=MESH,
        )
        copy.start()
        exchange.append(copy)

    for b in range(2 // batch):
        exchange[b].wait_recv()
        rows = []
        for n in range(2 * batch * b, 2 * batch * b + 2 * batch):
            o = other[n]
            crossed = jnp.where(real_lane, pltpu.roll(o, 96, 1), pltpu.roll(o, 32, 1))
            c = etab[0] * spec[n] + etab[1] * o + etab[2] * crossed
            rows += [c, pltpu.roll(c, 64, 1)]
        z = dot_right(jnp.concatenate(rows, axis=0), h)
        parts = []
        for n in range(4 * batch):
            re, im = z[n * 64:n * 64 + 64, :128], z[n * 64:n * 64 + 64, 128:]
            parts.append(jnp.concatenate([re * cos_t - im * sin_t, im * cos_t + re * sin_t], axis=0))
        wave = dot_left(f2, jnp.concatenate(parts, axis=1))
        for q in range(batch):
            qb = b * batch + q
            packed = []
            for k in range(3):
                coef = [jnp.where(left_half, mix_ref[k, 0, cl], mix_ref[k, 0, 2 + cl]) for cl in range(2)]
                mixed = []
                for qa in range(2):
                    at = [(q * 4 + cl * 2 + qa) * 128 for cl in range(2)]
                    v = coef[0] * wave[:, at[0]:at[0] + 128] + coef[1] * wave[:, at[1]:at[1] + 128]
                    mixed.append(v + pltpu.roll(v, 64, 1))
                packed.append(jnp.where(left_half, mixed[0], mixed[1]))
                usend[pl.ds(2 * k + qb, 64, stride=8), :] = packed[k]
            ph, plow = halves(jnp.concatenate(packed, axis=1))
            ends = mm(ph, pick[...]) + mm(plow, pick[...])
            edge.append(jnp.where(lane & 8 == 0, pltpu.roll(ends, 1, 0), pltpu.roll(ends, 63, 0)))

    usend[pl.ds(6, 64, stride=8), :] = jnp.where(lane < 16, edge[0], pltpu.roll(edge[1], 16, 1))

    special = jnp.where(first_slab, SECTORS - 1, 0)
    mine = jnp.where(me == SECTORS - 1 - special, 1, 0)

    def gather(j):
        pltpu.make_async_remote_copy(
            src_ref=tile(usend, j, 7), dst_ref=tile(out_u, me, 7), send_sem=usem, recv_sem=ursem.at[mine],
            device_id={"slab": 1 - slab, "sector": j}, device_id_type=MESH,
        ).start()

    each_peer(gather)

    for copy in halo2:
        copy.wait_recv()
    outs = [
        pltpu.make_async_copy(dinv.at[:, pl.ds(0, 2)], out_d, osem.at[0]),
        pltpu.make_async_copy(row2_r, out_r, osem.at[1]),
        pltpu.make_async_copy(col2_r, out_c, osem.at[2]),
        pltpu.make_async_copy(result, out_a, osem.at[3]),
    ]
    for copy in outs[:3]:
        copy.start()

    def sweep2(k, carry):
        new = relax(k, a1, row2_r, col2_r)
        for c in range(3):
            result[c, k] = new[c]
        return carry

    lax.fori_loop(0, LAYERS, sweep2, 0)
    outs[3].start()

    pltpu.make_async_copy(tile(usend, 0, 7), tile(out_u, 0, 7), ursem.at[1]).wait()
    forward = pltpu.make_async_remote_copy(
        src_ref=tile(out_u, special, 7), dst_ref=out_x.at[pl.ds(0, 7)], send_sem=xsem.at[0], recv_sem=xsem.at[1],
        device_id={"slab": 1 - slab}, device_id_type=MESH,
    )
    forward.start()
    pltpu.make_async_copy(usend.at[pl.ds(0, 441)], out_u.at[pl.ds(0, 441)], ursem.at[0]).wait()

    forward.wait_recv()
    pltpu.make_async_copy(wsend, rrecv, fsend).wait()
    pltpu.make_async_copy(usend.at[pl.ds(0, 448)], out_u.at[pl.ds(0, 448)], usem).wait()
    for copy in outs:
        copy.wait()
    for copy in halo1 + halo2 + exchange + [forward]:
        copy.wait_send()


def finish(a_hbm, u_hbm, x_hbm, d_hbm, r_hbm, c_hbm, out, result, urecv, xcol, dinv, rows, cols_r, isem, osem):
    first_slab = lax.axis_index("slab") == 0
    loads = [
        pltpu.make_async_copy(src, dst, isem.at[i])
        for i, (src, dst) in enumerate(((u_hbm, urecv), (d_hbm, dinv), (x_hbm, xcol), (r_hbm, rows), (c_hbm, cols_r)))
    ]
    layers = [pl.ds(k, 2) for k in range(0, LAYERS, 2)]
    loads += [pltpu.make_async_copy(a_hbm.at[:, k], result.at[:, k], isem.at[5 + i]) for i, k in enumerate(layers)]
    stores = [pltpu.make_async_copy(result.at[:, k], out.at[:, k], osem.at[i]) for i, k in enumerate(layers)]
    for copy in loads:
        copy.start()
    for i in range(1, 4):
        loads[5 + i].wait()
        stores[i].start()
    for copy in loads[:6]:
        copy.wait()

    def solve(k, y):
        return apply([dinv[i, k] for i in range(6)], y)

    turned = []
    for k in range(3):
        both = jnp.concatenate([urecv[pl.ds(2 * k + qb, 64, stride=8), :] for qb in range(2)], axis=0)
        turned.append(both.T)
    edge = urecv[pl.ds(6, 64, stride=8), :]
    turned.append(jnp.concatenate([edge, pltpu.roll(edge, 112, 1)], axis=0).T)
    source = [jnp.concatenate([turned[c][:64], turned[c][64:]], axis=1) for c in range(3)]
    src_prev = [jnp.concatenate([turned[3][c:c + 1], turned[3][4 + c:5 + c]], axis=1) for c in range(3)]
    src_next = [jnp.concatenate([turned[3][8 + c:9 + c], turned[3][12 + c:13 + c]], axis=1) for c in range(3)]
    delta = solve(0, source)

    delta_prev = apply([rows[0, 24 + i:25 + i, :] for i in range(6)], src_prev)
    delta_next = apply([rows[1, 24 + i:25 + i, :] for i in range(6)], src_next)
    cols = xcol[...].T
    cols = [jnp.where(first_slab, cols[:64, 2 * c:2 * c + 1], cols[64:, 2 * c + 1:2 * c + 2]) for c in range(3)]
    dcol = cols_r[...]
    delta_col = apply([dcol[:, 24 + i:25 + i] for i in range(6)], cols)
    y = [source[c] + beside(first_slab, delta[c], delta_prev[c], delta_next[c], delta_col[c]) for c in range(3)]
    low = solve(0, y)
    up = solve(1, delta)
    for c in range(3):
        result[c, 0] = result[c, 0] + low[c]
        result[c, 1] = result[c, 1] + up[c]
    stores[0].start()
    for copy in stores:
        copy.wait()


def shards(traces, gap_gain, rotor_step, mixing, field, current, cond_diag, cond_off):
    consts = [jnp.asarray(t) for t in tables()]
    hbm = pl.BlockSpec(memory_space=pltpu.HBM)
    block = (3, LAYERS, PHD, AXD)
    dma = pltpu.SemaphoreType.DMA
    v = pltpu.VMEM
    shapes = (block, (512, 128), (8, 128), (6, 2, 64, AXD), (2, 32, AXD), (64, 128))
    parts = pl.pallas_call(
        kernel,
        out_shape=[jax.ShapeDtypeStruct(shape, F32) for shape in shapes],
        in_specs=[hbm] * 14,
        out_specs=[hbm] * 6,
        scratch_shapes=[
            pltpu.SMEM((1, 1), jnp.int32), pltpu.SMEM((3, 1, 4), F32), v((8, 128), F32),
            v((64, 4, AXD), F32), v((3, LAYERS + 2, 64, AXD), F32), v(block, F32), v(block, F32), v(block, F32),
            v((2, 128, 64), BF16), v((2, 64, 128), BF16), v((2, 256, 128), BF16), v((2, 128, 256), BF16),
            v((2, 64, 128), F32), v((384, 128), BF16),
            v((6, LAYERS, 64, AXD), F32), v((3, LAYERS + 2, 64, AXD), F32), v(block, F32),
            v((512, 128), F32), v((512, 128), F32), v((512, 128), F32),
            v((4, 64, 128), F32), v((4, 64, 128), F32), v((3, 64, 128), F32),
            v((2, 24, AXD), F32), v((2, 24, AXD), F32), v((64, 128), F32), v((64, 128), F32),
            v((2, 32, AXD), F32), v((2, 32, AXD), F32), v((64, 128), F32), v((64, 128), F32),
            dma((14,)), dma, dma, dma, dma((2,)), dma((4,)), dma((4,)),
            dma((3,)), dma((3,)), dma((3,)), dma((3,)), dma((2,)), dma((4,)),
        ],
        compiler_params=pltpu.CompilerParams(collective_id=0, has_side_effects=True, vmem_limit_bytes=62 * 1024 * 1024),
        cost_estimate=pl.CostEstimate(flops=400_000_000, bytes_accessed=10_000_000, transcendentals=0),
    )(
        rotor_step.reshape(1, 1), jnp.transpose(mixing, (1, 0, 2)), gap_gain.reshape(8, 128), traces[0], field[0], current[0], cond_diag[0], cond_off[0],
        *consts,
    )
    out = pl.pallas_call(
        finish,
        out_shape=jax.ShapeDtypeStruct(block, F32),
        in_specs=[hbm] * 6,
        out_specs=hbm,
        scratch_shapes=[v(shape, F32) for shape in shapes] + [dma((9,)), dma((4,))],
        compiler_params=pltpu.CompilerParams(vmem_limit_bytes=62 * 1024 * 1024),
        cost_estimate=pl.CostEstimate(flops=10_000_000, bytes_accessed=4_200_000, transcendentals=0),
    )(*parts)
    return out[None]


def solution(mesh):
    placed = (
        P("side", "sector", None, "slab"),
        P(),
        P(),
        P("side", None, None),
        P("side", None, None, "sector", "slab"),
        P("side", None, None, "sector", "slab"),
        P("side", None, None, "sector", "slab"),
        P("side", None, None, "sector", "slab"),
    )
    return jax.shard_map(
        shards,
        mesh=mesh,
        in_specs=placed,
        out_specs=P("side", None, None, "sector", "slab"),
        check_vma=False,
    )
```

```python
import math

import jax
import jax.numpy as jnp
import ml_dtypes
import numpy as np
from jax import lax
from jax.experimental import pallas as pl
from jax.experimental.pallas import tpu as pltpu
from jax.sharding import PartitionSpec as P

SWEEPS = 2
MESH = pl.DeviceIdType.MESH
SECTORS = 64
PHD = 64
NPHI = 4096
M1 = 16
LAYERS = 8
AXD = 256
F32 = jnp.float32
BF16 = jnp.bfloat16


def split_table(table):
    high = table.astype(np.float32).astype(ml_dtypes.bfloat16)
    low = (table - high.astype(np.float64)).astype(np.float32).astype(ml_dtypes.bfloat16)
    return np.stack([high, low])


def tables():
    s = np.arange(SECTORS)
    m0 = np.arange(64)
    p = np.arange(PHD)
    m1 = np.arange(M1)
    a = 2.0 * np.pi * ((m0[:, None] * s[None, :]) % 64) / 64.0
    outer = np.concatenate([np.cos(a), -np.sin(a)], axis=0)
    b = 2.0 * np.pi * (m0[:, None] * p[None, :]) / NPHI
    twiddle = np.stack([np.tile(np.cos(b), (1, 2)), np.tile(np.sin(b), (1, 2))]).astype(np.float32)
    c = 2.0 * np.pi * ((p[:, None] * m1[None, :]) % 64) / 64.0
    cos_b = np.kron(np.eye(2), np.cos(c))
    sin_b = np.kron(np.eye(2), np.sin(c))
    inner = np.block([[cos_b, -sin_b], [sin_b, cos_b]])
    back = np.concatenate([inner.T, np.zeros((64, 256))], axis=0)
    pick = np.zeros((3 * 128, 128))
    for k in range(3):
        for qa in range(2):
            pick[k * 128 + qa * 64 + 63, qa * 4 + k] = 1.0
            pick[k * 128 + qa * 64, 8 + qa * 4 + k] = 1.0
    return (
        split_table(outer),
        split_table(np.ascontiguousarray(outer.T)),
        split_table(np.tile(inner, (1, 2))),
        split_table(back),
        twiddle,
        pick.astype(ml_dtypes.bfloat16),
    )


def halves(x):
    high = x.astype(BF16)
    return high, (x - high.astype(F32)).astype(BF16)


def mm(a, b):
    return jnp.dot(a, b, preferred_element_type=F32)


def dot_right(x, table):
    rows = x.shape[0]
    high, low = halves(x)
    both = mm(jnp.concatenate([high, low], axis=0), table[0])
    return both[:rows] + both[rows:] + mm(high, table[1])


def dot_left(table, x):
    high, low = halves(x)
    return mm(table[0], high) + mm(table[0], low) + mm(table[1], high)


def apply(d, y):
    return (
        d[0] * y[0] + d[1] * y[1] + d[2] * y[2],
        d[1] * y[0] + d[3] * y[1] + d[4] * y[2],
        d[2] * y[0] + d[4] * y[1] + d[5] * y[2],
    )


def beside(first_slab, x, prev_row, next_row, column):
    wide = lax.broadcasted_iota(jnp.int32, (64, AXD), 1)
    high = lax.broadcasted_iota(jnp.int32, (64, AXD), 0)
    up = jnp.where(high == 0, prev_row, pltpu.roll(x, 1, 0))
    down = jnp.where(high == 63, next_row, pltpu.roll(x, 63, 0))
    left = jnp.where(wide == 0, jnp.where(first_slab, 0.0, column), pltpu.roll(x, 1, 1))
    right = jnp.where(wide == AXD - 1, jnp.where(first_slab, column, 0.0), pltpu.roll(x, AXD - 1, 1))
    return up + down + (left + right)


def kernel(
    step_hbm, mix_hbm, gain_hbm, traces_hbm, field_hbm, current_hbm, diag_hbm, off_hbm,
    f1_hbm, f2_hbm, g_hbm, h_hbm, tw_hbm, pick_hbm,
    out_a, out_u, out_x, out_d, out_r, out_c,
    step_ref, mix_ref, gain_ref, traces, field, current, diag, off, f1, f2, g, h, tw, pick,
    dinv, a1, result, wsend, rrecv, usend, spec, other, etab,
    row_s, row_r, col_s, col_r, row2_s, row2_r, col2_s, col2_r,
    load, fsend, frecv, usem, ursem, ssend, srecv, hsend, hrecv, h2send, h2recv, xsem, osem,
):
    slab = lax.axis_index("slab")
    me = lax.axis_index("sector")
    side = lax.axis_index("side")
    nxt = lax.rem(me + 1, SECTORS)
    prv = lax.rem(me + SECTORS - 1, SECTORS)

    loads = [
        pltpu.make_async_copy(traces_hbm, traces, load.at[0]),
        pltpu.make_async_copy(field_hbm, field.at[:, pl.ds(1, LAYERS)], load.at[1]),
        pltpu.make_async_copy(diag_hbm, diag, load.at[2]),
        pltpu.make_async_copy(off_hbm, off, load.at[3]),
        pltpu.make_async_copy(current_hbm, current, load.at[4]),
        pltpu.make_async_copy(f1_hbm, f1, load.at[5]),
        pltpu.make_async_copy(f2_hbm, f2, load.at[6]),
        pltpu.make_async_copy(g_hbm, g, load.at[7]),
        pltpu.make_async_copy(h_hbm, h, load.at[8]),
        pltpu.make_async_copy(tw_hbm, tw, load.at[9]),
        pltpu.make_async_copy(pick_hbm, pick, load.at[10]),
        pltpu.make_async_copy(step_hbm, step_ref, load.at[11]),
        pltpu.make_async_copy(mix_hbm, mix_ref, load.at[12]),
        pltpu.make_async_copy(gain_hbm, gain_ref, load.at[13]),
    ]
    for copy in loads:
        copy.start()

    barrier = pltpu.get_barrier_semaphore()

    mx, mz, my = me >> 5, (me >> 2) & 7, me & 3
    corners = [x << 5 | (my + d) & 3 for d in (2, 1, 3, 0) for x in (mx, 1 - mx)]

    def each_peer(act):
        def ring(i, carry):
            for k in range(8):
                act((me + 18 + 8 * i + k) & 63)
            return carry

        lax.fori_loop(0, 8, ring, 0)

    def greet(j):
        pl.semaphore_signal(barrier, inc=1, device_id={"slab": 1 - slab, "sector": j}, device_id_type=MESH)

    each_peer(greet)
    pl.semaphore_signal(barrier, inc=1, device_id={"side": 1 - side}, device_id_type=MESH)
    pl.semaphore_signal(barrier, inc=1, device_id={"sector": nxt}, device_id_type=MESH)
    pl.semaphore_signal(barrier, inc=1, device_id={"sector": prv}, device_id_type=MESH)

    loads[0].wait()
    for cl in range(2):
        stacked = jnp.concatenate([traces[:, cl, :], traces[:, 2 + cl, :]], axis=0)
        for qa in range(2):
            turned = stacked[:, qa * 128:(qa + 1) * 128].T
            for qb in range(2):
                wsend[pl.ds(cl * 4 + qa * 2 + qb, 64, stride=8), :] = turned[qb * 64:(qb + 1) * 64]

    def tile(ref, j, rows=8):
        return ref.at[pl.ds(pl.multiple_of(j * 8, 8), rows)]

    lane = lax.broadcasted_iota(jnp.int32, (64, 128), 1)
    first_slab = slab == 0

    def edge_column(x):
        return jnp.where(first_slab, x[:, AXD - 1:AXD], x[:, 0:1])

    loads[1].wait()
    field[:, 0] = jnp.zeros((3, 64, AXD), F32)
    field[:, LAYERS + 1] = jnp.zeros((3, 64, AXD), F32)
    a1[:, 0] = jnp.zeros((3, 64, AXD), F32)
    a1[:, LAYERS + 1] = jnp.zeros((3, 64, AXD), F32)

    def edges(k, carry):
        columns = col_s[...]
        for c in range(3):
            x = field[c, k + 1]
            row_s[0, pl.ds(c * 8 + k, 1), :] = x[63:64]
            row_s[1, pl.ds(c * 8 + k, 1), :] = x[0:1]
            columns = jnp.where(lane == c * 8 + k, edge_column(x), columns)
        col_s[...] = columns
        return carry

    lax.fori_loop(0, LAYERS, edges, 0)

    def halo(rows_s, rows_r, cols_s, cols_r, send, recv):
        return [
            pltpu.make_async_remote_copy(
                src_ref=rows_s.at[0], dst_ref=rows_r.at[0], send_sem=send.at[0], recv_sem=recv.at[0],
                device_id={"sector": nxt}, device_id_type=MESH,
            ),
            pltpu.make_async_remote_copy(
                src_ref=rows_s.at[1], dst_ref=rows_r.at[1], send_sem=send.at[1], recv_sem=recv.at[1],
                device_id={"sector": prv}, device_id_type=MESH,
            ),
            pltpu.make_async_remote_copy(
                src_ref=cols_s, dst_ref=cols_r, send_sem=send.at[2], recv_sem=recv.at[2],
                device_id={"slab": 1 - slab}, device_id_type=MESH,
            ),
        ]

    pl.semaphore_wait(barrier, SECTORS + 3)

    halo1 = halo(row_s, row_r, col_s, col_r, hsend, hrecv)
    for copy in halo1:
        copy.start()

    def scatter(j):
        pltpu.make_async_remote_copy(
            src_ref=tile(wsend, j), dst_ref=tile(rrecv, me), send_sem=fsend, recv_sem=frecv,
            device_id={"slab": 1 - slab, "sector": j}, device_id_type=MESH,
        ).start()

    each_peer(scatter)

    loads[2].wait()
    loads[3].wait()

    def invert(k, carry):
        da = 6.0 + diag[0, k]
        db = 6.0 + diag[1, k]
        dc = 6.0 + diag[2, k]
        op, oq, orr = off[0, k], off[1, k], off[2, k]
        c00 = db * dc - orr * orr
        c01 = oq * orr - op * dc
        c02 = op * orr - oq * db
        c11 = da * dc - oq * oq
        c12 = op * oq - da * orr
        c22 = da * db - op * op
        inv = 1.0 / (da * c00 + op * c01 + oq * c02)
        for i, cof in enumerate((c00, c01, c02, c11, c12, c22)):
            dinv[i, k] = cof * inv
        return carry

    lax.fori_loop(0, LAYERS, invert, 0)

    def solve(k, y):
        return apply([dinv[i, k] for i in range(6)], y)

    def relax(k, src, rows_r, cols_r):
        y = []
        for c in range(3):
            x = src[c, k + 1]
            column = pltpu.roll(cols_r[...], 128 - c * 8 - k, 1)[:, 0:1]
            near = beside(first_slab, x, rows_r[0, pl.ds(c * 8 + k, 1), :], rows_r[1, pl.ds(c * 8 + k, 1), :], column)
            y.append(current[c, k] + (src[c, k] + src[c, k + 2] + near))
        return solve(k, y)

    for copy in halo1:
        copy.wait_recv()
    loads[4].wait()

    def sweep1(k, carry):
        new = relax(k, field, row_r, col_r)
        columns = col2_s[...]
        for c in range(3):
            a1[c, k + 1] = new[c]
            row2_s[0, pl.ds(c * 8 + k, 1), :] = new[c][63:64]
            row2_s[1, pl.ds(c * 8 + k, 1), :] = new[c][0:1]
            columns = jnp.where(lane == c * 8 + k, edge_column(new[c]), columns)
        col2_s[...] = columns
        return carry

    lax.fori_loop(0, LAYERS, sweep1, 0)
    columns = col2_s[...]
    for i in range(6):
        x = dinv[i, 0]
        row2_s[0, 24 + i:25 + i, :] = x[63:64]
        row2_s[1, 24 + i:25 + i, :] = x[0:1]
        columns = jnp.where(lane == 24 + i, edge_column(x), columns)
    col2_s[...] = columns
    halo2 = halo(row2_s, row2_r, col2_s, col2_r, h2send, h2recv)

    for copy in loads[11:]:
        copy.wait()

    m1 = lane % M1
    harm = lax.broadcasted_iota(jnp.int32, (64, 128), 0) + 64 * m1
    angle = (harm * step_ref[0, 0] % NPHI).astype(F32) * (2.0 * math.pi / NPHI)
    weight = jnp.where(harm == 0, 1.0 / NPHI, 2.0 / NPHI)
    turned = gain_ref[...].T
    gain = jnp.zeros((64, 128), F32)
    for i in range(8):
        gain = jnp.where(m1 == 2 * i, turned[:64, i:i + 1], gain)
        gain = jnp.where(m1 == 2 * i + 1, turned[64:, i:i + 1], gain)
    scaled = gain * weight
    sign = (2 * side - 1).astype(F32)
    etab[0] = weight
    etab[1] = scaled * jnp.cos(angle)
    etab[2] = scaled * jnp.sin(angle) * jnp.where(lane % 64 < 32, -sign, sign)

    for copy in loads[5:11]:
        copy.wait()
    pltpu.make_async_copy(wsend, rrecv, frecv).wait()
    for copy in halo2:
        copy.start()

    exchange = []
    edge = []
    cos_t, sin_t = tw[0], tw[1]
    left_half = lane < 64
    real_lane = lane % 64 < 32
    batch = 2
    for b in range(2 // batch):
        order = [(cl, qa, qb) for qb in range(batch * b, batch * b + batch) for cl in range(2) for qa in range(2)]
        x = jnp.concatenate([rrecv[pl.ds(cl * 4 + qa * 2 + qb, 64, stride=8), :] for cl, qa, qb in order], axis=1)
        y = dot_left(f1, x)
        rows = []
        for n in range(4 * batch):
            re, im = y[:64, n * 128:n * 128 + 128], y[64:, n * 128:n * 128 + 128]
            rows.append(jnp.concatenate([re * cos_t + im * sin_t, im * cos_t - re * sin_t], axis=1))
        both = dot_right(jnp.concatenate(rows, axis=0), g)
        for n in range(2 * batch):
            spec[2 * batch * b + n] = jnp.where(left_half, both[n * 128:n * 128 + 64], both[n * 128 + 64:n * 128 + 128])
        part = pl.ds(2 * batch * b, 2 * batch)
        copy = pltpu.make_async_remote_copy(
            src_ref=spec.at[part], dst_ref=other.at[part], send_sem=ssend.at[b], recv_sem=srecv.at[b],
            device_id={"side": 1 - side}, device_id_type=MESH,
        )
        copy.start()
        exchange.append(copy)

    for b in range(2 // batch):
        exchange[b].wait_recv()
        rows = []
        for n in range(2 * batch * b, 2 * batch * b + 2 * batch):
            o = other[n]
            crossed = jnp.where(real_lane, pltpu.roll(o, 96, 1), pltpu.roll(o, 32, 1))
            c = etab[0] * spec[n] + etab[1] * o + etab[2] * crossed
            rows += [c, pltpu.roll(c, 64, 1)]
        z = dot_right(jnp.concatenate(rows, axis=0), h)
        parts = []
        for n in range(4 * batch):
            re, im = z[n * 64:n * 64 + 64, :128], z[n * 64:n * 64 + 64, 128:]
            parts.append(jnp.concatenate([re * cos_t - im * sin_t, im * cos_t + re * sin_t], axis=0))
        wave = dot_left(f2, jnp.concatenate(parts, axis=1))
        for q in range(batch):
            qb = b * batch + q
            packed = []
            for k in range(3):
                coef = [jnp.where(left_half, mix_ref[k, 0, cl], mix_ref[k, 0, 2 + cl]) for cl in range(2)]
                mixed = []
                for qa in range(2):
                    at = [(q * 4 + cl * 2 + qa) * 128 for cl in range(2)]
                    v = coef[0] * wave[:, at[0]:at[0] + 128] + coef[1] * wave[:, at[1]:at[1] + 128]
                    mixed.append(v + pltpu.roll(v, 64, 1))
                packed.append(jnp.where(left_half, mixed[0], mixed[1]))
                usend[pl.ds(2 * k + qb, 64, stride=8), :] = packed[k]
            ph, plow = halves(jnp.concatenate(packed, axis=1))
            ends = mm(ph, pick[...]) + mm(plow, pick[...])
            edge.append(jnp.where(lane & 8 == 0, pltpu.roll(ends, 1, 0), pltpu.roll(ends, 63, 0)))

    usend[pl.ds(6, 64, stride=8), :] = jnp.where(lane < 16, edge[0], pltpu.roll(edge[1], 16, 1))

    special = jnp.where(first_slab, SECTORS - 1, 0)
    mine = jnp.where(me == SECTORS - 1 - special, 1, 0)

    def gather(j):
        pltpu.make_async_remote_copy(
            src_ref=tile(usend, j, 7), dst_ref=tile(out_u, me, 7), send_sem=usem, recv_sem=ursem.at[mine],
            device_id={"slab": 1 - slab, "sector": j}, device_id_type=MESH,
        ).start()

    each_peer(gather)

    for copy in halo2:
        copy.wait_recv()
    outs = [
        pltpu.make_async_copy(dinv.at[:, pl.ds(0, 2)], out_d, osem.at[0]),
        pltpu.make_async_copy(row2_r, out_r, osem.at[1]),
        pltpu.make_async_copy(col2_r, out_c, osem.at[2]),
        pltpu.make_async_copy(result, out_a, osem.at[3]),
    ]
    for copy in outs[:3]:
        copy.start()

    def sweep2(k, carry):
        new = relax(k, a1, row2_r, col2_r)
        for c in range(3):
            result[c, k] = new[c]
        return carry

    lax.fori_loop(0, LAYERS, sweep2, 0)
    outs[3].start()

    pltpu.make_async_copy(tile(usend, 0, 7), tile(out_u, 0, 7), ursem.at[1]).wait()
    forward = pltpu.make_async_remote_copy(
        src_ref=tile(out_u, special, 7), dst_ref=out_x.at[pl.ds(0, 7)], send_sem=xsem.at[0], recv_sem=xsem.at[1],
        device_id={"slab": 1 - slab}, device_id_type=MESH,
    )
    forward.start()
    pltpu.make_async_copy(usend.at[pl.ds(0, 441)], out_u.at[pl.ds(0, 441)], ursem.at[0]).wait()

    forward.wait_recv()
    pltpu.make_async_copy(wsend, rrecv, fsend).wait()
    pltpu.make_async_copy(usend.at[pl.ds(0, 448)], out_u.at[pl.ds(0, 448)], usem).wait()
    for copy in outs:
        copy.wait()
    for copy in halo1 + halo2 + exchange + [forward]:
        copy.wait_send()


def finish(a_hbm, u_hbm, x_hbm, d_hbm, r_hbm, c_hbm, out, result, urecv, xcol, dinv, rows, cols_r, isem, osem):
    first_slab = lax.axis_index("slab") == 0
    loads = [
        pltpu.make_async_copy(src, dst, isem.at[i])
        for i, (src, dst) in enumerate(((u_hbm, urecv), (d_hbm, dinv), (x_hbm, xcol), (r_hbm, rows), (c_hbm, cols_r)))
    ]
    layers = [pl.ds(0, 1), pl.ds(1, 1), pl.ds(2, 2), pl.ds(4, 2), pl.ds(6, 2)]
    loads += [pltpu.make_async_copy(a_hbm.at[:, k], result.at[:, k], isem.at[5 + i]) for i, k in enumerate(layers)]
    stores = [pltpu.make_async_copy(result.at[:, k], out.at[:, k], osem.at[i]) for i, k in enumerate(layers)]
    for copy in loads:
        copy.start()

    def solve(k, y):
        return apply([dinv[i, k] for i in range(6)], y)

    loads[0].wait()
    turned = []
    for k in range(3):
        both = jnp.concatenate([urecv[pl.ds(2 * k + qb, 64, stride=8), :] for qb in range(2)], axis=0)
        turned.append(both.T)
    edge = urecv[pl.ds(6, 64, stride=8), :]
    turned.append(jnp.concatenate([edge, pltpu.roll(edge, 112, 1)], axis=0).T)
    source = [jnp.concatenate([turned[c][:64], turned[c][64:]], axis=1) for c in range(3)]
    src_prev = [jnp.concatenate([turned[3][c:c + 1], turned[3][4 + c:5 + c]], axis=1) for c in range(3)]
    src_next = [jnp.concatenate([turned[3][8 + c:9 + c], turned[3][12 + c:13 + c]], axis=1) for c in range(3)]
    loads[1].wait()
    delta = solve(0, source)
    up = solve(1, delta)
    loads[6].wait()
    for c in range(3):
        result[c, 1] = result[c, 1] + up[c]
    stores[1].start()
    for i in range(2, 5):
        loads[5 + i].wait()
        stores[i].start()
    for copy in loads[2:6]:
        copy.wait()

    delta_prev = apply([rows[0, 24 + i:25 + i, :] for i in range(6)], src_prev)
    delta_next = apply([rows[1, 24 + i:25 + i, :] for i in range(6)], src_next)
    cols = xcol[...].T
    cols = [jnp.where(first_slab, cols[:64, 2 * c:2 * c + 1], cols[64:, 2 * c + 1:2 * c + 2]) for c in range(3)]
    dcol = cols_r[...]
    delta_col = apply([dcol[:, 24 + i:25 + i] for i in range(6)], cols)
    y = [source[c] + beside(first_slab, delta[c], delta_prev[c], delta_next[c], delta_col[c]) for c in range(3)]
    low = solve(0, y)
    for c in range(3):
        result[c, 0] = result[c, 0] + low[c]
    stores[0].start()
    for copy in stores:
        copy.wait()


def shards(traces, gap_gain, rotor_step, mixing, field, current, cond_diag, cond_off):
    consts = [jnp.asarray(t) for t in tables()]
    hbm = pl.BlockSpec(memory_space=pltpu.HBM)
    block = (3, LAYERS, PHD, AXD)
    dma = pltpu.SemaphoreType.DMA
    v = pltpu.VMEM
    shapes = (block, (512, 128), (8, 128), (6, 2, 64, AXD), (2, 32, AXD), (64, 128))
    parts = pl.pallas_call(
        kernel,
        out_shape=[jax.ShapeDtypeStruct(shape, F32) for shape in shapes],
        in_specs=[hbm] * 14,
        out_specs=[hbm] * 6,
        scratch_shapes=[
            pltpu.SMEM((1, 1), jnp.int32), pltpu.SMEM((3, 1, 4), F32), v((8, 128), F32),
            v((64, 4, AXD), F32), v((3, LAYERS + 2, 64, AXD), F32), v(block, F32), v(block, F32), v(block, F32),
            v((2, 128, 64), BF16), v((2, 64, 128), BF16), v((2, 256, 128), BF16), v((2, 128, 256), BF16),
            v((2, 64, 128), F32), v((384, 128), BF16),
            v((6, LAYERS, 64, AXD), F32), v((3, LAYERS + 2, 64, AXD), F32), v(block, F32),
            v((512, 128), F32), v((512, 128), F32), v((512, 128), F32),
            v((4, 64, 128), F32), v((4, 64, 128), F32), v((3, 64, 128), F32),
            v((2, 24, AXD), F32), v((2, 24, AXD), F32), v((64, 128), F32), v((64, 128), F32),
            v((2, 32, AXD), F32), v((2, 32, AXD), F32), v((64, 128), F32), v((64, 128), F32),
            dma((14,)), dma, dma, dma, dma((2,)), dma((4,)), dma((4,)),
            dma((3,)), dma((3,)), dma((3,)), dma((3,)), dma((2,)), dma((4,)),
        ],
        compiler_params=pltpu.CompilerParams(collective_id=0, has_side_effects=True, vmem_limit_bytes=62 * 1024 * 1024),
        cost_estimate=pl.CostEstimate(flops=400_000_000, bytes_accessed=10_000_000, transcendentals=0),
    )(
        rotor_step.reshape(1, 1), jnp.transpose(mixing, (1, 0, 2)), gap_gain.reshape(8, 128), traces[0], field[0], current[0], cond_diag[0], cond_off[0],
        *consts,
    )
    out = pl.pallas_call(
        finish,
        out_shape=jax.ShapeDtypeStruct(block, F32),
        in_specs=[hbm] * 6,
        out_specs=hbm,
        scratch_shapes=[v(shape, F32) for shape in shapes] + [dma((10,)), dma((5,))],
        compiler_params=pltpu.CompilerParams(vmem_limit_bytes=62 * 1024 * 1024),
        cost_estimate=pl.CostEstimate(flops=10_000_000, bytes_accessed=4_200_000, transcendentals=0),
    )(*parts)
    return out[None]


def solution(mesh):
    placed = (
        P("side", "sector", None, "slab"),
        P(),
        P(),
        P("side", None, None),
        P("side", None, None, "sector", "slab"),
        P("side", None, None, "sector", "slab"),
        P("side", None, None, "sector", "slab"),
        P("side", None, None, "sector", "slab"),
    )
    return jax.shard_map(
        shards,
        mesh=mesh,
        in_specs=placed,
        out_specs=P("side", None, None, "sector", "slab"),
        check_vma=False,
    )
```

```python
import math

import jax
import jax.numpy as jnp
import ml_dtypes
import numpy as np
from jax import lax
from jax.experimental import pallas as pl
from jax.experimental.pallas import tpu as pltpu
from jax.sharding import PartitionSpec as P

SWEEPS = 2
MESH = pl.DeviceIdType.MESH
SECTORS = 64
PHD = 64
NPHI = 4096
M1 = 16
LAYERS = 8
AXD = 256
F32 = jnp.float32
BF16 = jnp.bfloat16


def split_table(table):
    high = table.astype(np.float32).astype(ml_dtypes.bfloat16)
    low = (table - high.astype(np.float64)).astype(np.float32).astype(ml_dtypes.bfloat16)
    return np.stack([high, low])


def tables():
    s = np.arange(SECTORS)
    m0 = np.arange(64)
    p = np.arange(PHD)
    m1 = np.arange(M1)
    a = 2.0 * np.pi * ((m0[:, None] * s[None, :]) % 64) / 64.0
    outer = np.concatenate([np.cos(a), -np.sin(a)], axis=0)
    b = 2.0 * np.pi * (m0[:, None] * p[None, :]) / NPHI
    twiddle = np.stack([np.tile(np.cos(b), (1, 2)), np.tile(np.sin(b), (1, 2))]).astype(np.float32)
    c = 2.0 * np.pi * ((p[:, None] * m1[None, :]) % 64) / 64.0
    cos_b = np.kron(np.eye(2), np.cos(c))
    sin_b = np.kron(np.eye(2), np.sin(c))
    inner = np.block([[cos_b, -sin_b], [sin_b, cos_b]])
    back = np.concatenate([inner.T, np.zeros((64, 256))], axis=0)
    pick = np.zeros((3 * 128, 128))
    for k in range(3):
        for qa in range(2):
            pick[k * 128 + qa * 64 + 63, qa * 4 + k] = 1.0
            pick[k * 128 + qa * 64, 8 + qa * 4 + k] = 1.0
    return (
        split_table(outer),
        split_table(np.ascontiguousarray(outer.T)),
        split_table(np.tile(inner, (1, 2))),
        split_table(back),
        twiddle,
        pick.astype(ml_dtypes.bfloat16),
    )


def halves(x):
    high = x.astype(BF16)
    return high, (x - high.astype(F32)).astype(BF16)


def mm(a, b):
    return jnp.dot(a, b, preferred_element_type=F32)


def dot_right(x, table):
    rows = x.shape[0]
    high, low = halves(x)
    both = mm(jnp.concatenate([high, low], axis=0), table[0])
    return both[:rows] + both[rows:] + mm(high, table[1])


def dot_left(table, x):
    high, low = halves(x)
    return mm(table[0], high) + mm(table[0], low) + mm(table[1], high)


def apply(d, y):
    return (
        d[0] * y[0] + d[1] * y[1] + d[2] * y[2],
        d[1] * y[0] + d[3] * y[1] + d[4] * y[2],
        d[2] * y[0] + d[4] * y[1] + d[5] * y[2],
    )


def beside(first_slab, x, prev_row, next_row, column):
    wide = lax.broadcasted_iota(jnp.int32, (64, AXD), 1)
    high = lax.broadcasted_iota(jnp.int32, (64, AXD), 0)
    up = jnp.where(high == 0, prev_row, pltpu.roll(x, 1, 0))
    down = jnp.where(high == 63, next_row, pltpu.roll(x, 63, 0))
    left = jnp.where(wide == 0, jnp.where(first_slab, 0.0, column), pltpu.roll(x, 1, 1))
    right = jnp.where(wide == AXD - 1, jnp.where(first_slab, column, 0.0), pltpu.roll(x, AXD - 1, 1))
    return up + down + (left + right)


def kernel(
    step_hbm, mix_hbm, gain_hbm, traces_hbm, field_hbm, current_hbm, diag_hbm, off_hbm,
    f1_hbm, f2_hbm, g_hbm, h_hbm, tw_hbm, pick_hbm,
    out_a, out_u, out_x, out_d, out_r, out_c,
    step_ref, mix_ref, gain_ref, traces, field, current, diag, off, f1, f2, g, h, tw, pick,
    dinv, a1, result, wsend, rrecv, usend, spec, other, etab,
    row_s, row_r, col_s, col_r, row2_s, row2_r, col2_s, col2_r,
    load, fsend, frecv, usem, ursem, ssend, srecv, hsend, hrecv, h2send, h2recv, xsem, osem,
):
    slab = lax.axis_index("slab")
    me = lax.axis_index("sector")
    side = lax.axis_index("side")
    nxt = lax.rem(me + 1, SECTORS)
    prv = lax.rem(me + SECTORS - 1, SECTORS)

    loads = [
        pltpu.make_async_copy(traces_hbm, traces, load.at[0]),
        pltpu.make_async_copy(field_hbm, field.at[:, pl.ds(1, LAYERS)], load.at[1]),
        pltpu.make_async_copy(diag_hbm, diag, load.at[2]),
        pltpu.make_async_copy(off_hbm, off, load.at[3]),
        pltpu.make_async_copy(current_hbm, current, load.at[4]),
        pltpu.make_async_copy(f1_hbm, f1, load.at[5]),
        pltpu.make_async_copy(f2_hbm, f2, load.at[6]),
        pltpu.make_async_copy(g_hbm, g, load.at[7]),
        pltpu.make_async_copy(h_hbm, h, load.at[8]),
        pltpu.make_async_copy(tw_hbm, tw, load.at[9]),
        pltpu.make_async_copy(pick_hbm, pick, load.at[10]),
        pltpu.make_async_copy(step_hbm, step_ref, load.at[11]),
        pltpu.make_async_copy(mix_hbm, mix_ref, load.at[12]),
        pltpu.make_async_copy(gain_hbm, gain_ref, load.at[13]),
    ]
    for copy in loads:
        copy.start()

    barrier = pltpu.get_barrier_semaphore()

    mx, mz, my = me >> 5, (me >> 2) & 7, me & 3
    corners = [x << 5 | (my + d) & 3 for d in (2, 1, 3, 0) for x in (mx, 1 - mx)]

    def each_peer(act):
        def ring(i, carry):
            for k in range(8):
                act((me + 8 * i + k) & 63)
            return carry

        lax.fori_loop(0, 8, ring, 0)

    def greet(j):
        pl.semaphore_signal(barrier, inc=1, device_id={"slab": 1 - slab, "sector": j}, device_id_type=MESH)

    each_peer(greet)
    pl.semaphore_signal(barrier, inc=1, device_id={"side": 1 - side}, device_id_type=MESH)
    pl.semaphore_signal(barrier, inc=1, device_id={"sector": nxt}, device_id_type=MESH)
    pl.semaphore_signal(barrier, inc=1, device_id={"sector": prv}, device_id_type=MESH)

    loads[0].wait()
    for cl in range(2):
        stacked = jnp.concatenate([traces[:, cl, :], traces[:, 2 + cl, :]], axis=0)
        for qa in range(2):
            turned = stacked[:, qa * 128:(qa + 1) * 128].T
            for qb in range(2):
                wsend[pl.ds(cl * 4 + qa * 2 + qb, 64, stride=8), :] = turned[qb * 64:(qb + 1) * 64]

    def tile(ref, j, rows=8):
        return ref.at[pl.ds(pl.multiple_of(j * 8, 8), rows)]

    lane = lax.broadcasted_iota(jnp.int32, (64, 128), 1)
    first_slab = slab == 0

    def edge_column(x):
        return jnp.where(first_slab, x[:, AXD - 1:AXD], x[:, 0:1])

    loads[1].wait()
    field[:, 0] = jnp.zeros((3, 64, AXD), F32)
    field[:, LAYERS + 1] = jnp.zeros((3, 64, AXD), F32)
    a1[:, 0] = jnp.zeros((3, 64, AXD), F32)
    a1[:, LAYERS + 1] = jnp.zeros((3, 64, AXD), F32)

    def edges(k, carry):
        columns = col_s[...]
        for c in range(3):
            x = field[c, k + 1]
            row_s[0, pl.ds(c * 8 + k, 1), :] = x[63:64]
            row_s[1, pl.ds(c * 8 + k, 1), :] = x[0:1]
            columns = jnp.where(lane == c * 8 + k, edge_column(x), columns)
        col_s[...] = columns
        return carry

    lax.fori_loop(0, LAYERS, edges, 0)

    def halo(rows_s, rows_r, cols_s, cols_r, send, recv):
        return [
            pltpu.make_async_remote_copy(
                src_ref=rows_s.at[0], dst_ref=rows_r.at[0], send_sem=send.at[0], recv_sem=recv.at[0],
                device_id={"sector": nxt}, device_id_type=MESH,
            ),
            pltpu.make_async_remote_copy(
                src_ref=rows_s.at[1], dst_ref=rows_r.at[1], send_sem=send.at[1], recv_sem=recv.at[1],
                device_id={"sector": prv}, device_id_type=MESH,
            ),
            pltpu.make_async_remote_copy(
                src_ref=cols_s, dst_ref=cols_r, send_sem=send.at[2], recv_sem=recv.at[2],
                device_id={"slab": 1 - slab}, device_id_type=MESH,
            ),
        ]

    pl.semaphore_wait(barrier, SECTORS + 3)

    halo1 = halo(row_s, row_r, col_s, col_r, hsend, hrecv)
    for copy in halo1:
        copy.start()

    def scatter(j):
        pltpu.make_async_remote_copy(
            src_ref=tile(wsend, j), dst_ref=tile(rrecv, me), send_sem=fsend, recv_sem=frecv,
            device_id={"slab": 1 - slab, "sector": j}, device_id_type=MESH,
        ).start()

    each_peer(scatter)

    loads[2].wait()
    loads[3].wait()

    def invert(k, carry):
        da = 6.0 + diag[0, k]
        db = 6.0 + diag[1, k]
        dc = 6.0 + diag[2, k]
        op, oq, orr = off[0, k], off[1, k], off[2, k]
        c00 = db * dc - orr * orr
        c01 = oq * orr - op * dc
        c02 = op * orr - oq * db
        c11 = da * dc - oq * oq
        c12 = op * oq - da * orr
        c22 = da * db - op * op
        inv = 1.0 / (da * c00 + op * c01 + oq * c02)
        for i, cof in enumerate((c00, c01, c02, c11, c12, c22)):
            dinv[i, k] = cof * inv
        return carry

    lax.fori_loop(0, LAYERS, invert, 0)

    def solve(k, y):
        return apply([dinv[i, k] for i in range(6)], y)

    def relax(k, src, rows_r, cols_r):
        y = []
        for c in range(3):
            x = src[c, k + 1]
            column = pltpu.roll(cols_r[...], 128 - c * 8 - k, 1)[:, 0:1]
            near = beside(first_slab, x, rows_r[0, pl.ds(c * 8 + k, 1), :], rows_r[1, pl.ds(c * 8 + k, 1), :], column)
            y.append(current[c, k] + (src[c, k] + src[c, k + 2] + near))
        return solve(k, y)

    for copy in halo1:
        copy.wait_recv()
    loads[4].wait()

    def sweep1(k, carry):
        new = relax(k, field, row_r, col_r)
        columns = col2_s[...]
        for c in range(3):
            a1[c, k + 1] = new[c]
            row2_s[0, pl.ds(c * 8 + k, 1), :] = new[c][63:64]
            row2_s[1, pl.ds(c * 8 + k, 1), :] = new[c][0:1]
            columns = jnp.where(lane == c * 8 + k, edge_column(new[c]), columns)
        col2_s[...] = columns
        return carry

    lax.fori_loop(0, LAYERS, sweep1, 0)
    columns = col2_s[...]
    for i in range(6):
        x = dinv[i, 0]
        row2_s[0, 24 + i:25 + i, :] = x[63:64]
        row2_s[1, 24 + i:25 + i, :] = x[0:1]
        columns = jnp.where(lane == 24 + i, edge_column(x), columns)
    col2_s[...] = columns
    halo2 = halo(row2_s, row2_r, col2_s, col2_r, h2send, h2recv)

    for copy in loads[11:]:
        copy.wait()

    m1 = lane % M1
    harm = lax.broadcasted_iota(jnp.int32, (64, 128), 0) + 64 * m1
    angle = (harm * step_ref[0, 0] % NPHI).astype(F32) * (2.0 * math.pi / NPHI)
    weight = jnp.where(harm == 0, 1.0 / NPHI, 2.0 / NPHI)
    turned = gain_ref[...].T
    gain = jnp.zeros((64, 128), F32)
    for i in range(8):
        gain = jnp.where(m1 == 2 * i, turned[:64, i:i + 1], gain)
        gain = jnp.where(m1 == 2 * i + 1, turned[64:, i:i + 1], gain)
    scaled = gain * weight
    sign = (2 * side - 1).astype(F32)
    etab[0] = weight
    etab[1] = scaled * jnp.cos(angle)
    etab[2] = scaled * jnp.sin(angle) * jnp.where(lane % 64 < 32, -sign, sign)

    for copy in loads[5:11]:
        copy.wait()
    pltpu.make_async_copy(wsend, rrecv, frecv).wait()
    for copy in halo2:
        copy.start()

    exchange = []
    edge = []
    cos_t, sin_t = tw[0], tw[1]
    left_half = lane < 64
    real_lane = lane % 64 < 32
    batch = 2
    for b in range(2 // batch):
        order = [(cl, qa, qb) for qb in range(batch * b, batch * b + batch) for cl in range(2) for qa in range(2)]
        x = jnp.concatenate([rrecv[pl.ds(cl * 4 + qa * 2 + qb, 64, stride=8), :] for cl, qa, qb in order], axis=1)
        y = dot_left(f1, x)
        rows = []
        for n in range(4 * batch):
            re, im = y[:64, n * 128:n * 128 + 128], y[64:, n * 128:n * 128 + 128]
            rows.append(jnp.concatenate([re * cos_t + im * sin_t, im * cos_t - re * sin_t], axis=1))
        both = dot_right(jnp.concatenate(rows, axis=0), g)
        for n in range(2 * batch):
            spec[2 * batch * b + n] = jnp.where(left_half, both[n * 128:n * 128 + 64], both[n * 128 + 64:n * 128 + 128])
        part = pl.ds(2 * batch * b, 2 * batch)
        copy = pltpu.make_async_remote_copy(
            src_ref=spec.at[part], dst_ref=other.at[part], send_sem=ssend.at[b], recv_sem=srecv.at[b],
            device_id={"side": 1 - side}, device_id_type=MESH,
        )
        copy.start()
        exchange.append(copy)

    for b in range(2 // batch):
        exchange[b].wait_recv()
        rows = []
        for n in range(2 * batch * b, 2 * batch * b + 2 * batch):
            o = other[n]
            crossed = jnp.where(real_lane, pltpu.roll(o, 96, 1), pltpu.roll(o, 32, 1))
            c = etab[0] * spec[n] + etab[1] * o + etab[2] * crossed
            rows += [c, pltpu.roll(c, 64, 1)]
        z = dot_right(jnp.concatenate(rows, axis=0), h)
        parts = []
        for n in range(4 * batch):
            re, im = z[n * 64:n * 64 + 64, :128], z[n * 64:n * 64 + 64, 128:]
            parts.append(jnp.concatenate([re * cos_t - im * sin_t, im * cos_t + re * sin_t], axis=0))
        wave = dot_left(f2, jnp.concatenate(parts, axis=1))
        for q in range(batch):
            qb = b * batch + q
            packed = []
            for k in range(3):
                coef = [jnp.where(left_half, mix_ref[k, 0, cl], mix_ref[k, 0, 2 + cl]) for cl in range(2)]
                mixed = []
                for qa in range(2):
                    at = [(q * 4 + cl * 2 + qa) * 128 for cl in range(2)]
                    v = coef[0] * wave[:, at[0]:at[0] + 128] + coef[1] * wave[:, at[1]:at[1] + 128]
                    mixed.append(v + pltpu.roll(v, 64, 1))
                packed.append(jnp.where(left_half, mixed[0], mixed[1]))
                usend[pl.ds(2 * k + qb, 64, stride=8), :] = packed[k]
            ph, plow = halves(jnp.concatenate(packed, axis=1))
            ends = mm(ph, pick[...]) + mm(plow, pick[...])
            edge.append(jnp.where(lane & 8 == 0, pltpu.roll(ends, 1, 0), pltpu.roll(ends, 63, 0)))

    usend[pl.ds(6, 64, stride=8), :] = jnp.where(lane < 16, edge[0], pltpu.roll(edge[1], 16, 1))

    special = jnp.where(first_slab, SECTORS - 1, 0)
    mine = jnp.where(me == SECTORS - 1 - special, 1, 0)

    def gather(j):
        pltpu.make_async_remote_copy(
            src_ref=tile(usend, j, 7), dst_ref=tile(out_u, me, 7), send_sem=usem, recv_sem=ursem.at[mine],
            device_id={"slab": 1 - slab, "sector": j}, device_id_type=MESH,
        ).start()

    each_peer(gather)

    for copy in halo2:
        copy.wait_recv()
    outs = [
        pltpu.make_async_copy(dinv.at[:, pl.ds(0, 2)], out_d, osem.at[0]),
        pltpu.make_async_copy(row2_r, out_r, osem.at[1]),
        pltpu.make_async_copy(col2_r, out_c, osem.at[2]),
        pltpu.make_async_copy(result, out_a, osem.at[3]),
    ]
    for copy in outs[:3]:
        copy.start()

    def sweep2(k, carry):
        new = relax(k, a1, row2_r, col2_r)
        for c in range(3):
            result[c, k] = new[c]
        return carry

    lax.fori_loop(0, LAYERS, sweep2, 0)
    outs[3].start()

    pltpu.make_async_copy(tile(usend, 0, 7), tile(out_u, 0, 7), ursem.at[1]).wait()
    forward = pltpu.make_async_remote_copy(
        src_ref=tile(out_u, special, 7), dst_ref=out_x.at[pl.ds(0, 7)], send_sem=xsem.at[0], recv_sem=xsem.at[1],
        device_id={"slab": 1 - slab}, device_id_type=MESH,
    )
    forward.start()
    pltpu.make_async_copy(usend.at[pl.ds(0, 441)], out_u.at[pl.ds(0, 441)], ursem.at[0]).wait()

    forward.wait_recv()
    pltpu.make_async_copy(wsend, rrecv, fsend).wait()
    pltpu.make_async_copy(usend.at[pl.ds(0, 448)], out_u.at[pl.ds(0, 448)], usem).wait()
    for copy in outs:
        copy.wait()
    for copy in halo1 + halo2 + exchange + [forward]:
        copy.wait_send()


def finish(a_hbm, u_hbm, x_hbm, d_hbm, r_hbm, c_hbm, out, result, urecv, xcol, dinv, rows, cols_r, isem, osem):
    first_slab = lax.axis_index("slab") == 0
    loads = [
        pltpu.make_async_copy(src, dst, isem.at[i])
        for i, (src, dst) in enumerate(((u_hbm, urecv), (d_hbm, dinv), (x_hbm, xcol), (r_hbm, rows), (c_hbm, cols_r)))
    ]
    layers = [pl.ds(0, 1), pl.ds(1, 1), pl.ds(2, 2), pl.ds(4, 2), pl.ds(6, 2)]
    loads += [pltpu.make_async_copy(a_hbm.at[:, k], result.at[:, k], isem.at[5 + i]) for i, k in enumerate(layers)]
    stores = [pltpu.make_async_copy(result.at[:, k], out.at[:, k], osem.at[i]) for i, k in enumerate(layers)]
    for copy in loads:
        copy.start()

    def solve(k, y):
        return apply([dinv[i, k] for i in range(6)], y)

    loads[0].wait()
    turned = []
    for k in range(3):
        both = jnp.concatenate([urecv[pl.ds(2 * k + qb, 64, stride=8), :] for qb in range(2)], axis=0)
        turned.append(both.T)
    edge = urecv[pl.ds(6, 64, stride=8), :]
    turned.append(jnp.concatenate([edge, pltpu.roll(edge, 112, 1)], axis=0).T)
    source = [jnp.concatenate([turned[c][:64], turned[c][64:]], axis=1) for c in range(3)]
    src_prev = [jnp.concatenate([turned[3][c:c + 1], turned[3][4 + c:5 + c]], axis=1) for c in range(3)]
    src_next = [jnp.concatenate([turned[3][8 + c:9 + c], turned[3][12 + c:13 + c]], axis=1) for c in range(3)]
    loads[1].wait()
    delta = solve(0, source)
    up = solve(1, delta)
    loads[6].wait()
    for c in range(3):
        result[c, 1] = result[c, 1] + up[c]
    stores[1].start()
    for i in range(2, 5):
        loads[5 + i].wait()
        stores[i].start()
    for copy in loads[2:6]:
        copy.wait()

    delta_prev = apply([rows[0, 24 + i:25 + i, :] for i in range(6)], src_prev)
    delta_next = apply([rows[1, 24 + i:25 + i, :] for i in range(6)], src_next)
    cols = xcol[...].T
    cols = [jnp.where(first_slab, cols[:64, 2 * c:2 * c + 1], cols[64:, 2 * c + 1:2 * c + 2]) for c in range(3)]
    dcol = cols_r[...]
    delta_col = apply([dcol[:, 24 + i:25 + i] for i in range(6)], cols)
    y = [source[c] + beside(first_slab, delta[c], delta_prev[c], delta_next[c], delta_col[c]) for c in range(3)]
    low = solve(0, y)
    for c in range(3):
        result[c, 0] = result[c, 0] + low[c]
    stores[0].start()
    for copy in stores:
        copy.wait()


def shards(traces, gap_gain, rotor_step, mixing, field, current, cond_diag, cond_off):
    consts = [jnp.asarray(t) for t in tables()]
    hbm = pl.BlockSpec(memory_space=pltpu.HBM)
    block = (3, LAYERS, PHD, AXD)
    dma = pltpu.SemaphoreType.DMA
    v = pltpu.VMEM
    shapes = (block, (512, 128), (8, 128), (6, 2, 64, AXD), (2, 32, AXD), (64, 128))
    parts = pl.pallas_call(
        kernel,
        out_shape=[jax.ShapeDtypeStruct(shape, F32) for shape in shapes],
        in_specs=[hbm] * 14,
        out_specs=[hbm] * 6,
        scratch_shapes=[
            pltpu.SMEM((1, 1), jnp.int32), pltpu.SMEM((3, 1, 4), F32), v((8, 128), F32),
            v((64, 4, AXD), F32), v((3, LAYERS + 2, 64, AXD), F32), v(block, F32), v(block, F32), v(block, F32),
            v((2, 128, 64), BF16), v((2, 64, 128), BF16), v((2, 256, 128), BF16), v((2, 128, 256), BF16),
            v((2, 64, 128), F32), v((384, 128), BF16),
            v((6, LAYERS, 64, AXD), F32), v((3, LAYERS + 2, 64, AXD), F32), v(block, F32),
            v((512, 128), F32), v((512, 128), F32), v((512, 128), F32),
            v((4, 64, 128), F32), v((4, 64, 128), F32), v((3, 64, 128), F32),
            v((2, 24, AXD), F32), v((2, 24, AXD), F32), v((64, 128), F32), v((64, 128), F32),
            v((2, 32, AXD), F32), v((2, 32, AXD), F32), v((64, 128), F32), v((64, 128), F32),
            dma((14,)), dma, dma, dma, dma((2,)), dma((4,)), dma((4,)),
            dma((3,)), dma((3,)), dma((3,)), dma((3,)), dma((2,)), dma((4,)),
        ],
        compiler_params=pltpu.CompilerParams(collective_id=0, has_side_effects=True, vmem_limit_bytes=62 * 1024 * 1024),
        cost_estimate=pl.CostEstimate(flops=400_000_000, bytes_accessed=10_000_000, transcendentals=0),
    )(
        rotor_step.reshape(1, 1), jnp.transpose(mixing, (1, 0, 2)), gap_gain.reshape(8, 128), traces[0], field[0], current[0], cond_diag[0], cond_off[0],
        *consts,
    )
    out = pl.pallas_call(
        finish,
        out_shape=jax.ShapeDtypeStruct(block, F32),
        in_specs=[hbm] * 6,
        out_specs=hbm,
        scratch_shapes=[v(shape, F32) for shape in shapes] + [dma((10,)), dma((5,))],
        compiler_params=pltpu.CompilerParams(vmem_limit_bytes=62 * 1024 * 1024),
        cost_estimate=pl.CostEstimate(flops=10_000_000, bytes_accessed=4_200_000, transcendentals=0),
    )(*parts)
    return out[None]


def solution(mesh):
    placed = (
        P("side", "sector", None, "slab"),
        P(),
        P(),
        P("side", None, None),
        P("side", None, None, "sector", "slab"),
        P("side", None, None, "sector", "slab"),
        P("side", None, None, "sector", "slab"),
        P("side", None, None, "sector", "slab"),
    )
    return jax.shard_map(
        shards,
        mesh=mesh,
        in_specs=placed,
        out_specs=P("side", None, None, "sector", "slab"),
        check_vma=False,
    )
```
